256 devices in a mesh: frame: 16 (over z_lo, x, core), cam: 16 (over z_hi, y).
Axes of the slice: x: 4, y: 4, z: 8 (z_hi: 4, z_lo: 2; z = z_hi * 2 + z_lo), core: 2. Of those that a mesh axis runs over, the one named last changes fastest.
Arguments:
- view_maps: bfloat16 [32, 176, 2, 32, 256], P('frame', 'cam'), may hold values from -6 to 6
- conv_weight: bfloat16 [9, 256, 256], replicated, may hold values from -0.125 to 0.125
- join_weight: bfloat16 [16384, 256], P('cam'), may hold values from -0.1875 to 0.1875
- valid_cams: int32 [32, 176], P('frame'), may hold values from 0 to 1, as said below
- latent_grad: bfloat16 [32, 256], P('frame'), may hold values from -6 to 6
Outputs:
- latent: float32 [32, 256], P('frame')
- conv_grad: float32 [9, 256, 256], replicated
- join_grad: float32 [16384, 256], P(('cam', 'frame'))
The draws below stay inside these ranges and needn't reach their ends.
Inputs may be any that keep to these rules, and one draw needn't show every extreme that they name: `valid_cams`: every frame has at least one usable camera; the last 6 cameras are padding and never usable.
All inputs are finite; a program needn't handle non-finite values.
Results may differ from the reference program's by a relative error of at most 0.007.
Values may be sent and summed in bfloat16 or wider, within the bound.
No kernel may reach another device: no remote copies, remote signals or barrier semaphores. Data moves between devices by JAX's collectives and lax.ppermute only.
A program may use at most 64 MiB of HBM per device.

```python
import jax
import jax.numpy as jnp
from jax import lax

CH = 256
LAT = 256
COLS = 32
ROWS = 2
FRAMES = 32
CAMS = 176
FEAT = 16384


def draw_valid_cams(key, part):
    coin_key = jax.random.fold_in(key, 11)
    pick_key = jax.random.fold_in(key, 23)
    coins = jax.random.randint(coin_key, (FRAMES, CAMS), 0, 4)
    cam_index = jnp.arange(CAMS, dtype=jnp.int32)[None, :]
    usable = jnp.logical_and(coins > 0, cam_index < CAMS - 6)
    forced = jax.random.randint(pick_key, (FRAMES, 1), 0, CAMS - 6)
    chosen = jnp.logical_or(usable, cam_index == forced)
    return chosen.astype(jnp.int32)


def level_of(rng, extent, cuts, least, top_value):
    level, own = 1.0, jax.random.fold_in(rng, 6)
    for dim, parts in cuts:
        draws = jnp.exp(jax.random.uniform(jax.random.fold_in(own, dim), (parts,), jnp.float32, least / len(cuts), top_value / len(cuts)))
        level = level * jnp.repeat(draws, extent[dim] // parts).reshape([-1 if axis == dim else 1 for axis in range(len(extent))])
    return level


def gaussian(stream_key, shape, width, reach, shards=(), kind=jnp.bfloat16):
    array = jax.random.normal(stream_key, shape, jnp.float32) * width
    if len(shards) > 0:
        array = level_of(stream_key, shape, shards, -0.22, 0.18) * array
    return jnp.clip(array, min=-reach, max=reach).astype(kind)


def setup_inputs(seed: int = 0) -> dict:
    seeds = jax.random.split(jax.random.key(seed), 6)
    return {
        "view_maps": gaussian(seeds[0], (FRAMES, CAMS, ROWS, COLS, CH), 1.0, 6.0, ((0, 16), (1, 16))),
        "conv_weight": gaussian(seeds[1], (9, CH, CH), (9 * CH) ** -0.5, 0.125),
        "join_weight": gaussian(seeds[2], (FEAT, LAT), (FEAT // 16) ** -0.5, 0.1875, ((0, 16),)),
        "valid_cams": draw_valid_cams(jax.random.fold_in(seeds[5], 71), 0),
        "latent_grad": gaussian(seeds[4], (FRAMES, LAT), 1.0, 6.0, ((0, 16),)),
    }


def make_shifts(maps):
    padded = jnp.pad(maps, ((0, 0), (1, 1), (1, 1), (0, 0)))
    return [padded[:, dy:dy + ROWS, dx:dx + COLS, :].reshape(-1, CH) for dy in range(3) for dx in range(3)]


def reference(view_maps, conv_weight, join_weight, valid_cams, latent_grad):
    def frame_step(carry, inputs):
        conv_acc, join_acc = carry
        maps, valid_row, grad_row = inputs
        shifted = make_shifts(maps)
        preact = jnp.zeros((CAMS * ROWS * COLS, CH), jnp.float32)
        for k in range(9):
            preact = preact + jnp.dot(shifted[k], conv_weight[k], preferred_element_type=jnp.float32)
        sigma = jax.nn.sigmoid(preact)
        features = (preact * sigma).astype(jnp.bfloat16).reshape(CAMS, FEAT)
        mask_f = valid_row.astype(jnp.float32)
        cam_count = jnp.sum(mask_f)
        pooled = jnp.sum(mask_f[:, None] * features.astype(jnp.float32), axis=0)
        joined = (pooled / cam_count).astype(jnp.bfloat16)
        latent_row = jnp.dot(joined, join_weight, preferred_element_type=jnp.float32)
        joined_grad = jnp.dot(join_weight, grad_row, preferred_element_type=jnp.float32).astype(jnp.bfloat16)
        slopes = (sigma * (1.0 + preact * (1.0 - sigma))).reshape(CAMS, FEAT)
        weighting = mask_f / cam_count
        pre_grad = (joined_grad.astype(jnp.float32)[None, :] * weighting[:, None] * slopes).astype(jnp.bfloat16)
        pre_grad = pre_grad.reshape(-1, CH)
        taps = jnp.stack([jnp.dot(shifted[k].T, pre_grad, preferred_element_type=jnp.float32) for k in range(9)])
        conv_acc = conv_acc + taps
        join_acc = join_acc + jnp.outer(joined.astype(jnp.float32), grad_row.astype(jnp.float32))
        return (conv_acc, join_acc), latent_row

    start_carry = (jnp.zeros((9, CH, CH), jnp.float32), jnp.zeros((FEAT, LAT), jnp.float32))
    (conv_grad, join_grad), latent = lax.scan(frame_step, start_carry, (view_maps, valid_cams, latent_grad))
    return latent, conv_grad, join_grad
```

```python
import functools

import jax
import jax.numpy as jnp
from jax import lax
from jax.experimental import pallas as pl
from jax.experimental.pallas import tpu as pltpu
from jax.sharding import Mesh, PartitionSpec as P

BF = jnp.bfloat16
F32 = jnp.float32
CHIPS = ("zh", "y", "zl", "x")
SWAP = [(0, 1), (1, 0)]
N_CHIPS = 128
KDIM = 768

VM = pl.BlockSpec(memory_space=pltpu.VMEM)
SM = pl.BlockSpec(memory_space=pltpu.SMEM)


def params():
    return pltpu.CompilerParams(vmem_limit_bytes=48 * 1024 * 1024)


def dot(a, b):
    return jnp.dot(a, b, preferred_element_type=F32)


def joined_grad_kernel(grad_ref, join_ref, out_ref, rows):
    grad = grad_ref[...]
    for pos in range(4):
        part = lax.dot_general(
            grad, join_ref[256 * pos : 256 * pos + 256, :], (((1,), (1,)), ((), ())), preferred_element_type=F32
        )
        rows[pos : pos + 1, :] = part[0:1]
        rows[pos + 4 : pos + 5, :] = part[1:2]
    block = rows[...].astype(BF)
    out_ref[...] = jnp.broadcast_to(block[None], out_ref.shape)


def edge_masks(rows):
    column = lax.broadcasted_iota(jnp.int32, (rows, 256), 0) % 32
    return column != 0, column != 31


def forward_kernel(core_ref, weight_ref, maps_ref, conv_ref, pooled_ref, slope_ref, turned_ref):
    n = 11 * 32
    not_first, not_last = edge_masks(n)

    def frame(f, carry):
        at = f * 11
        top = maps_ref[pl.ds(at, 11), 0:32, :].reshape(n, 256)
        low = maps_ref[pl.ds(at, 11), 32:64, :].reshape(n, 256)
        for r in range(2):
            taps = [
                dot(top, conv_ref[(1 - r) * 3 + dx]) + dot(low, conv_ref[(2 - r) * 3 + dx])
                for dx in range(3)
            ]
            pre = taps[1]
            pre = pre + jnp.where(not_first, pltpu.roll(taps[0], 1, 0), 0.0)
            pre = pre + jnp.where(not_last, pltpu.roll(taps[2], n - 1, 0), 0.0)
            sigma = jax.nn.sigmoid(pre)
            feature = pre * sigma
            slope = sigma * (1.0 + pre * (1.0 - sigma))
            pooled = jnp.zeros((32, 256), F32)
            for c in range(11):
                weight = weight_ref[f, c]
                rows = slice(32 * c, 32 * c + 32)
                pooled = pooled + feature[rows] * weight
                slope_ref[at + c, 32 * r : 32 * r + 32, :] = slope[rows] * weight
            pooled_ref[f, 32 * r : 32 * r + 32, :] = pooled
        return carry

    lax.fori_loop(0, 2, frame, 0)

    core = core_ref[0]
    m = 22 * 32
    keep_first, keep_last = edge_masks(m)
    for r in range(2):
        rows = maps_ref[:, 32 * r : 32 * r + 32, :].reshape(m, 256).astype(F32)
        for dx in range(3):
            if dx == 0:
                shifted = jnp.where(keep_first, pltpu.roll(rows, 1, 0), 0.0)
            elif dx == 1:
                shifted = rows
            else:
                shifted = jnp.where(keep_last, pltpu.roll(rows, m - 1, 0), 0.0)
            shifted = jnp.concatenate([shifted, jnp.zeros((KDIM - m, 256), F32)], 0)
            turned = shifted.T.astype(BF)
            for half in range(2):
                slot = core if half == 0 else 1 - core
                start = pl.multiple_of(slot * 384 + dx * 128, 128)
                turned_ref[r, pl.ds(start, 128), :] = turned[128 * half : 128 * half + 128]


def backward_kernel(grad_ref, slope_ref, turned_ref, mine_ref, send_ref, grads, acc):
    for k in range(16):
        block = grad_ref[k].astype(F32)
        for f in range(2):
            grads[f, 4 * k : 4 * k + 4, :] = block[4 * f : 4 * f + 4]
    pre = []
    for r in range(2):
        parts = []
        for f in range(2):
            rows = grads[f, 32 * r : 32 * r + 32, :]
            slope = slope_ref[11 * f : 11 * f + 11, 32 * r : 32 * r + 32, :]
            parts.append((slope * rows[None]).reshape(352, 256).astype(BF))
        parts.append(jnp.zeros((KDIM - 704, 256), BF))
        pre.append(jnp.concatenate(parts, 0))

    def put(dy, value):
        for slot, ref in enumerate((mine_ref, send_ref)):
            for dx in range(3):
                for h in range(2):
                    s = (dy * 3 + dx) * 2 + h
                    ref[128 * s : 128 * s + 128, :] = value[
                        slot * 384 + dx * 128 : slot * 384 + dx * 128 + 128, 128 * h : 128 * h + 128
                    ].astype(ref.dtype)

    put(0, dot(turned_ref[0], pre[1]))
    put(1, dot(turned_ref[0], pre[0]) + dot(turned_ref[1], pre[1]))
    put(2, dot(turned_ref[1], pre[0]))


def pack_kernel(mine_ref, got_ref, pooled_ref, grad_ref, out_ref, tail):
    total = mine_ref[...] + got_ref[...].astype(F32)
    out_ref[:, 0:16, :] = total[0:2048].reshape(128, 16, 128).astype(BF)
    grad = grad_ref[...].astype(F32)
    for h in range(2):
        lanes = slice(128 * h, 128 * h + 128)
        tail[pl.ds(h, 128, stride=8), :] = total[2048 + 128 * h : 2176 + 128 * h]
        for j in range(2):
            tail[pl.ds(2 + j + 8 * h, 64, stride=16), :] = pooled_ref[j, :, lanes]
            tail[pl.ds(4 + 2 * j + h, 128, stride=8), :] = jnp.broadcast_to(grad[j : j + 1, lanes], (128, 128))
    out_ref[:, 16:24, :] = tail[...].reshape(128, 8, 128).astype(BF)


def reduce_kernel(got_ref, join_ref, out_ref, rest_ref, few):
    conv_a = jnp.sum(got_ref[:, 0:16, :].astype(F32), axis=0)
    tail = got_ref[:, 16:24, :].astype(F32)
    by_chip = jnp.sum(tail.reshape(16, 8, 8, 128), axis=0)
    few[...] = by_chip.reshape(64, 128)
    conv_b = jnp.sum(by_chip, axis=0)
    joined = [few[pl.ds(2 + j, 8, stride=8), :].astype(BF) for j in range(2)]
    few[...] = tail[0:8].reshape(64, 128)
    for j in range(2):
        rest_ref[j, :, 0:128] = joined[j]
        for h in range(2):
            rest_ref[j, :, 128 + 128 * h : 256 + 128 * h] = few[pl.ds(4 + 2 * j + h, 8, stride=8), :].astype(BF)
    few[...] = jnp.broadcast_to(conv_b[None], (8, 8, 128)).reshape(64, 128)
    for j in range(2):
        latent = dot(joined[j], join_ref[...])
        for h in range(2):
            few[pl.ds(2 + 2 * j + h, 8, stride=8), :] = latent[:, 128 * h : 128 * h + 128]
    out_ref[:, 0:16, :] = jnp.broadcast_to(conv_a.astype(BF)[None], (128, 16, 128))
    end = few[...].reshape(8, 8, 128).astype(BF)
    for k in range(16):
        out_ref[8 * k : 8 * k + 8, 16:24, :] = end


def spread_kernel(core_ref, own_ref, other_ref, conv_ref, latent_ref, tail):
    core = core_ref[0]
    for ref, half in ((own_ref, core), (other_ref, 1 - core)):
        start = pl.multiple_of(half * 128, 128)
        for s in range(16):
            slab = ref[8 * s : 8 * s + 8, 0:16, :].astype(F32).reshape(128, 128)
            lanes = slice(128 * (s % 2), 128 * (s % 2) + 128)
            conv_ref[s // 2, pl.ds(start, 128), lanes] = slab
        end = ref[:, 16:24, :].astype(F32)
        tail[...] = end.reshape(1024, 128)
        for h in range(2):
            conv_ref[8, pl.ds(start, 128), 128 * h : 128 * h + 128] = tail[pl.ds(h, 128, stride=8), :]
        if ref is own_ref:
            total = jnp.sum(end, axis=0)
            for j in range(2):
                for h in range(2):
                    row = 2 + 2 * j + h
                    latent_ref[j : j + 1, 128 * h : 128 * h + 128] = total[row : row + 1]


def shape(*dims, dtype=F32):
    return jax.ShapeDtypeStruct(dims, dtype)


def cost(flops, bytes_accessed):
    return pl.CostEstimate(flops=flops, bytes_accessed=bytes_accessed, transcendentals=0)


def on_device(view_maps, conv_weight, join_weight, valid_cams, latent_grad):
    core = lax.axis_index("c").astype(jnp.int32)
    cam = lax.axis_index(("zh", "y"))
    line = lax.axis_index(("zl", "x"))

    with jax.named_scope("joined_grad"):
        sent = pl.pallas_call(
            joined_grad_kernel,
            out_shape=shape(16, 8, 256, dtype=BF),
            in_specs=[VM, VM],
            out_specs=VM,
            scratch_shapes=[pltpu.VMEM((8, 256), F32)],
            compiler_params=params(),
            cost_estimate=cost(1 << 20, 600_000),
            name="joined_grad",
        )(latent_grad, join_weight)
        joined_grad = lax.all_to_all(sent, ("zh", "y"), 0, 0)

    with jax.named_scope("weights"):
        count = jnp.sum(valid_cams.astype(F32), axis=1)
        usable = lax.dynamic_slice_in_dim(valid_cams, cam * 11, 11, 1).astype(F32)
        weight = usable / count[:, None]
        join_rows = lax.dynamic_slice_in_dim(join_weight, line * 128, 128, 0)
        core_at = core.reshape(1)

    with jax.named_scope("forward"):
        pooled, slope, turned = pl.pallas_call(
            forward_kernel,
            out_shape=[shape(2, 64, 256), shape(22, 64, 256), shape(2, 768, KDIM, dtype=BF)],
            in_specs=[SM, SM, VM, VM],
            out_specs=[VM, VM, VM],
            compiler_params=params(),
            cost_estimate=cost(1_200_000_000, 6_000_000),
            name="forward",
        )(core_at, weight, view_maps.reshape(22, 64, 256), conv_weight)

    with jax.named_scope("backward"):
        mine, send = pl.pallas_call(
            backward_kernel,
            out_shape=[shape(2304, 128), shape(2304, 128, dtype=BF)],
            in_specs=[VM, VM, VM],
            out_specs=[VM, VM],
            scratch_shapes=[pltpu.VMEM((2, 64, 256), F32), pltpu.VMEM((8, 128), F32)],
            compiler_params=params(),
            cost_estimate=cost(1_200_000_000, 6_000_000),
            name="backward",
        )(joined_grad, slope, turned)

    with jax.named_scope("conv_scatter"):
        got = lax.ppermute(send, "c", SWAP)
        packed = pl.pallas_call(
            pack_kernel,
            out_shape=shape(N_CHIPS, 24, 128, dtype=BF),
            in_specs=[VM, VM, VM, VM],
            out_specs=VM,
            scratch_shapes=[pltpu.VMEM((1024, 128), F32)],
            compiler_params=params(),
            cost_estimate=cost(1_000_000, 3_000_000),
            name="pack",
        )(mine, got, pooled, latent_grad)
        blocks = lax.all_to_all(packed, CHIPS, 0, 0)

    with jax.named_scope("reduce"):
        summed, rest = pl.pallas_call(
            reduce_kernel,
            out_shape=[shape(N_CHIPS, 24, 128, dtype=BF), shape(2, 8, 384, dtype=BF)],
            in_specs=[VM, VM],
            out_specs=[VM, VM],
            scratch_shapes=[pltpu.VMEM((64, 128), F32)],
            compiler_params=params(),
            cost_estimate=cost(1_000_000, 3_000_000),
            name="reduce",
        )(blocks, join_rows)

    with jax.named_scope("conv_gather"):
        own = lax.all_to_all(summed, CHIPS, 0, 0)
        other = lax.ppermute(own, "c", SWAP)
        conv_grad, latent = pl.pallas_call(
            spread_kernel,
            out_shape=[shape(9, 256, 256), shape(2, 256)],
            in_specs=[SM, VM, VM],
            out_specs=[VM, VM],
            scratch_shapes=[pltpu.VMEM((1024, 128), F32)],
            compiler_params=params(),
            cost_estimate=cost(1_000_000, 4_000_000),
            name="spread",
        )(core_at, own, other)

    with jax.named_scope("join_grad"):
        rest_other = lax.ppermute(rest, "c", SWAP)
        both = jnp.concatenate([rest, rest_other], 0).reshape(32, 384)
        rows = lax.dynamic_slice_in_dim(both, core * 64, 64, 1)
        join_grad = lax.dot_general(rows, both[:, 128:], (((0,), (0,)), ((), ())), preferred_element_type=F32)
    return (latent, conv_grad, join_grad)


def solution(mesh):
    fine = Mesh(mesh.devices.reshape(2, 4, 2, 4, 4), ("zl", "x", "c", "zh", "y"))
    frame, cam = ("zl", "x", "c"), ("zh", "y")
    in_specs = (
        P(frame, cam, None, None, None),
        P(),
        P(cam, None),
        P(frame, None),
        P(frame, None),
    )
    out_specs = (P(frame, None), P(), P(cam + frame, None))
    return jax.shard_map(on_device, mesh=fine, in_specs=in_specs, out_specs=out_specs, check_vma=False)
```

```python
import functools

import jax
import jax.numpy as jnp
from jax import lax
from jax.experimental import pallas as pl
from jax.experimental.pallas import tpu as pltpu
from jax.sharding import Mesh, PartitionSpec as P

BF = jnp.bfloat16
F32 = jnp.float32
SWAP = [(0, 1), (1, 0)]
KDIM = 768

VM = pl.BlockSpec(memory_space=pltpu.VMEM)
SM = pl.BlockSpec(memory_space=pltpu.SMEM)
HBM = pl.BlockSpec(memory_space=pltpu.HBM)


def params():
    return pltpu.CompilerParams(vmem_limit_bytes=48 * 1024 * 1024)


def dot(a, b):
    return jnp.dot(a, b, preferred_element_type=F32)


def edge_masks(rows):
    column = lax.broadcasted_iota(jnp.int32, (rows, 256), 0) % 32
    return column != 0, column != 31


def forward_kernel(
    place_ref, valid_hbm, grad_hbm, join_hbm, maps_hbm, conv_hbm,
    out_ref, slope_ref, turned_ref,
    valid_ref, grad_ref, join_ref, maps_ref, conv_ref, rows_ref, sems,
):
    loads = [
        pltpu.make_async_copy(source, target, sems.at[i])
        for i, (source, target) in enumerate(
            (
                (valid_hbm, valid_ref),
                (grad_hbm, grad_ref),
                (join_hbm, join_ref),
                (maps_hbm, maps_ref),
                (conv_hbm, conv_ref),
            )
        )
    ]
    for load in loads:
        load.start()
    core, cam = place_ref[0], place_ref[1]
    loads[0].wait()
    valid = valid_ref[...].astype(F32)
    count = jnp.sum(valid, axis=1, keepdims=True)
    lane = lax.broadcasted_iota(jnp.int32, (2, 176), 1)
    weight = [jnp.sum(jnp.where(lane == cam * 11 + c, valid, 0.0), axis=1, keepdims=True) / count for c in range(11)]
    n = 11 * 32
    not_first, not_last = edge_masks(n)

    loads[1].wait()
    loads[2].wait()
    grad = grad_ref[...]
    for pos in range(4):
        part = lax.dot_general(
            grad, join_ref[256 * pos : 256 * pos + 256, :], (((1,), (1,)), ((), ())), preferred_element_type=F32
        )
        for j in range(2):
            rows_ref[4 * j + pos : 4 * j + pos + 1, :] = part[j : j + 1]
    out_ref[:, 0:8, :] = jnp.broadcast_to(rows_ref[0:8, :].astype(BF)[None], (16, 8, 256))

    loads[3].wait()
    loads[4].wait()
    for f in range(2):
        at = f * 11
        top = maps_ref[at : at + 11, 0:32, :].reshape(n, 256)
        low = maps_ref[at : at + 11, 32:64, :].reshape(n, 256)
        for r in range(2):
            taps = [
                dot(top, conv_ref[(1 - r) * 3 + dx]) + dot(low, conv_ref[(2 - r) * 3 + dx])
                for dx in range(3)
            ]
            pre = taps[1]
            pre = pre + jnp.where(not_first, pltpu.roll(taps[0], 1, 0), 0.0)
            pre = pre + jnp.where(not_last, pltpu.roll(taps[2], n - 1, 0), 0.0)
            sigma = jax.nn.sigmoid(pre)
            feature = pre * sigma
            slope = sigma * (1.0 + pre * (1.0 - sigma))
            pooled = jnp.zeros((32, 256), F32)
            for c in range(11):
                scale = weight[c][f : f + 1]
                rows = slice(32 * c, 32 * c + 32)
                pooled = pooled + feature[rows] * scale
                slope_ref[at + c, 32 * r : 32 * r + 32, :] = slope[rows] * scale
            for k in range(8):
                start = 8 * (8 * r + k) + 4 * f
                rows_ref[start : start + 4, :] = pooled[4 * k : 4 * k + 4]
    out_ref[:, 8:16, :] = rows_ref[...].reshape(16, 8, 256).astype(BF)

    m = 22 * 32
    keep_first, keep_last = edge_masks(m)
    for r in range(2):
        rows = maps_ref[:, 32 * r : 32 * r + 32, :].reshape(m, 256).astype(F32)
        for dx in range(3):
            if dx == 0:
                shifted = jnp.where(keep_first, pltpu.roll(rows, 1, 0), 0.0)
            elif dx == 1:
                shifted = rows
            else:
                shifted = jnp.where(keep_last, pltpu.roll(rows, m - 1, 0), 0.0)
            shifted = jnp.concatenate([shifted, jnp.zeros((KDIM - m, 256), F32)], 0)
            turned = shifted.T.astype(BF)
            for half in range(2):
                slot = core if half == 0 else 1 - core
                start = pl.multiple_of(slot * 384 + dx * 128, 128)
                turned_ref[r, pl.ds(start, 128), :] = turned[128 * half : 128 * half + 128]


def backward_kernel(grad_ref, slope_ref, turned_ref, mine_ref, send_ref, grads):
    for k in range(16):
        block = grad_ref[k, 0:8, :].astype(F32)
        for f in range(2):
            grads[f, 4 * k : 4 * k + 4, :] = block[4 * f : 4 * f + 4]
    pre = []
    for r in range(2):
        parts = []
        for f in range(2):
            rows = grads[f, 32 * r : 32 * r + 32, :]
            slope = slope_ref[11 * f : 11 * f + 11, 32 * r : 32 * r + 32, :]
            parts.append((slope * rows[None]).reshape(352, 256).astype(BF))
        parts.append(jnp.zeros((KDIM - 704, 256), BF))
        pre.append(jnp.concatenate(parts, 0))

    def put(dy, value):
        for slot, ref in enumerate((mine_ref, send_ref)):
            for dx in range(3):
                for h in range(2):
                    s = (dy * 3 + dx) * 2 + h
                    ref[128 * s : 128 * s + 128, :] = value[
                        slot * 384 + dx * 128 : slot * 384 + dx * 128 + 128, 128 * h : 128 * h + 128
                    ].astype(ref.dtype)

    put(0, dot(turned_ref[0], pre[1]))
    put(1, dot(turned_ref[0], pre[0]) + dot(turned_ref[1], pre[1]))
    put(2, dot(turned_ref[1], pre[0]))


def join_kernel(got_ref, join_ref, joined_ref, latent_ref):
    pooled = jnp.sum(got_ref[:, 8:16, :].astype(F32), axis=0)
    joined = pooled.astype(BF)
    joined_ref[...] = joined.astype(F32)
    parts = [dot(joined, join_ref[256 * pos : 256 * pos + 256, :]) for pos in range(4)]
    for j in range(2):
        latent_ref[j : j + 1, :] = sum(parts[pos][4 * j + pos : 4 * j + pos + 1] for pos in range(4))


def pack_kernel(place_ref, mine_ref, got_ref, joined_ref, latent_ref, grad_ref, out_ref, tail):
    total = (mine_ref[...] + got_ref[...].astype(F32)).astype(BF)
    out_ref[:, 0:144, :] = total.reshape(16, 144, 128)
    grad = grad_ref[...].astype(F32)
    tail[...] = jnp.zeros((16, 128), F32)
    for j in range(2):
        for h in range(2):
            tail[5 + 2 * j + h : 6 + 2 * j + h, :] = grad[j : j + 1, 128 * h : 128 * h + 128]
    for x in range(4):
        own = jnp.where(place_ref[2] == x, 1.0, 0.0)
        for j in range(2):
            for z in range(2):
                t = 4 * z + x
                row = 4 * j + t // 2
                lanes = slice(128 * (t % 2), 128 * (t % 2) + 128)
                tail[1 + 2 * j + z : 2 + 2 * j + z, :] = joined_ref[row : row + 1, lanes]
        for y in range(4):
            tail[0:1, :] = latent_ref[y // 2 : y // 2 + 1, 128 * (y % 2) : 128 * (y % 2) + 128] * own
            out_ref[4 * x + y, 144:160, :] = tail[...].astype(BF)


def middle_kernel(place_ref, got_ref, out_ref, ends):
    own_y = place_ref[3]
    conv = jnp.sum(got_ref[:, 0:144, :].astype(F32), axis=0)
    end = jnp.sum(got_ref[:, 144:160, :].astype(F32), axis=0)
    ends[...] = jnp.zeros((2, 32, 128), F32)
    for x in range(4):
        block = got_ref[4 * x + own_y, 144:160, :].astype(F32)
        for z in range(2):
            for j in range(2):
                ends[z, 1 + 2 * x + j : 2 + 2 * x + j, :] = block[1 + 2 * j + z : 2 + 2 * j + z]
            ends[z, 9 + 4 * x : 13 + 4 * x, :] = block[5:9]
    for z in range(2):
        ends[z, 0:1, :] = end[0:1]
    conv = conv.astype(BF)
    for z in range(8):
        out_ref[z, 0:144, :] = conv
        out_ref[z, 144:176, :] = ends[z % 2].astype(BF)


def finish_kernel(place_ref, got_ref, out_ref, rest_ref, rows_ref):
    own_high, own_low = place_ref[4], place_ref[5]
    conv = jnp.sum(got_ref[:, 0:144, :].astype(F32), axis=0).astype(BF)
    latent = jnp.zeros((8, 128), F32)
    for z in range(4):
        latent = latent + got_ref[2 * z + own_low, 144:176, :].astype(F32)[0:8]
    latent = latent.astype(BF)
    for k in range(16):
        out_ref[k, 0:144, :] = conv
        out_ref[k, 144:152, :] = latent
    for z in range(2):
        block = got_ref[2 * own_high + z, 144:176, :].astype(F32)
        rows_ref[8 * z : 8 * z + 8, 0:128] = block[1:9]
        for x in range(4):
            for j in range(2):
                for h in range(2):
                    row = 9 + 4 * x + 2 * j + h
                    at = 8 * z + 2 * x + j
                    rows_ref[at : at + 1, 128 + 128 * h : 256 + 128 * h] = block[row : row + 1]
    rest_ref[...] = rows_ref[...].astype(BF)


def spread_kernel(place_ref, own_ref, other_ref, conv_ref, latent_ref):
    core, own_x = place_ref[0], place_ref[2]
    for ref, half in ((own_ref, core), (other_ref, 1 - core)):
        for g in range(144):
            s, i = g // 8, 16 * (g % 8)
            start = pl.multiple_of(half * 128 + i, 16)
            lanes = slice(128 * (s % 2), 128 * (s % 2) + 128)
            offset = 16 * (g % 9)
            conv_ref[s // 2, pl.ds(start, 16), lanes] = ref[g // 9, offset : offset + 16, :].astype(F32)
    for y in range(4):
        row = own_ref[4 * own_x + y, 144:152, :].astype(F32)[0:1]
        latent_ref[y // 2 : y // 2 + 1, 128 * (y % 2) : 128 * (y % 2) + 128] = row


def shape(*dims, dtype=F32):
    return jax.ShapeDtypeStruct(dims, dtype)


def call(kernel, name, out_shape, in_specs, scratch=(), flops=1_000_000, moved=3_000_000):
    return pl.pallas_call(
        kernel,
        out_shape=out_shape,
        in_specs=in_specs,
        out_specs=[VM] * len(out_shape),
        scratch_shapes=scratch,
        compiler_params=params(),
        cost_estimate=pl.CostEstimate(flops=flops, bytes_accessed=moved, transcendentals=0),
        name=name,
    )


def on_device(view_maps, conv_weight, join_weight, valid_cams, latent_grad):
    names = ("c", ("zh", "y"), "x", "y", "zh", "zl")
    place = jnp.stack([lax.axis_index(name).astype(jnp.int32) for name in names])

    with jax.named_scope("forward"):
        shares, slope, turned = call(
            forward_kernel,
            "forward",
            [shape(16, 16, 256, dtype=BF), shape(22, 64, 256), shape(2, 768, KDIM, dtype=BF)],
            [SM, HBM, HBM, HBM, HBM, HBM],
            [
                pltpu.VMEM((2, 176), jnp.int32),
                pltpu.VMEM((2, 256), BF),
                pltpu.VMEM((1024, 256), BF),
                pltpu.VMEM((22, 64, 256), BF),
                pltpu.VMEM((9, 256, 256), BF),
                pltpu.VMEM((128, 256), F32),
                pltpu.SemaphoreType.DMA((5,)),
            ],
            flops=1_200_000_000,
        )(place, valid_cams, latent_grad, join_weight, view_maps.reshape(22, 64, 256), conv_weight)
        cam_shares = lax.all_to_all(shares, ("zh", "y"), 0, 0)

    with jax.named_scope("backward"):
        mine, send = call(
            backward_kernel,
            "backward",
            [shape(2304, 128), shape(2304, 128, dtype=BF)],
            [VM, VM, VM],
            [pltpu.VMEM((2, 64, 256), F32)],
            flops=1_200_000_000,
        )(cam_shares, slope, turned)
        got = lax.ppermute(send, "c", SWAP)

    with jax.named_scope("join"):
        joined, latent_part = call(join_kernel, "join", [shape(8, 256), shape(2, 256)], [VM, VM])(
            cam_shares, join_weight
        )

    with jax.named_scope("conv_scatter"):
        (packed,) = call(
            pack_kernel,
            "pack",
            [shape(16, 160, 128, dtype=BF)],
            [SM, VM, VM, VM, VM, VM],
            [pltpu.VMEM((16, 128), F32)],
        )(place, mine, got, joined, latent_part, latent_grad)
        blocks = lax.all_to_all(packed, ("x", "y"), 0, 0)

    with jax.named_scope("conv_middle"):
        (middle,) = call(
            middle_kernel, "middle", [shape(8, 176, 128, dtype=BF)], [SM, VM], [pltpu.VMEM((2, 32, 128), F32)]
        )(place, blocks)
        lines = lax.all_to_all(middle, ("zh", "zl"), 0, 0)

    with jax.named_scope("conv_gather"):
        summed, rest = call(
            finish_kernel,
            "finish",
            [shape(16, 152, 128, dtype=BF), shape(16, 384, dtype=BF)],
            [SM, VM],
            [pltpu.VMEM((16, 384), F32)],
        )(place, lines)
        own = lax.all_to_all(summed, ("x", "y"), 0, 0)
        other = lax.ppermute(own, "c", SWAP)
        conv_grad, latent = call(spread_kernel, "spread", [shape(9, 256, 256), shape(2, 256)], [SM, VM, VM])(
            place, own, other
        )

    with jax.named_scope("join_grad"):
        rest_other = lax.ppermute(rest, "c", SWAP)
        both = jnp.concatenate([rest, rest_other], 0)
        rows = lax.dynamic_slice_in_dim(both, place[0] * 64, 64, 1)
        join_grad = lax.dot_general(rows, both[:, 128:], (((0,), (0,)), ((), ())), preferred_element_type=F32)
    return (latent, conv_grad, join_grad)


def solution(mesh):
    fine = Mesh(mesh.devices.reshape(2, 4, 2, 4, 4), ("zl", "x", "c", "zh", "y"))
    frame, cam = ("zl", "x", "c"), ("zh", "y")
    in_specs = (
        P(frame, cam, None, None, None),
        P(),
        P(cam, None),
        P(frame, None),
        P(frame, None),
    )
    out_specs = (P(frame, None), P(), P(cam + frame, None))
    return jax.shard_map(on_device, mesh=fine, in_specs=in_specs, out_specs=out_specs, check_vma=False)
```

```python
import functools

import jax
import jax.numpy as jnp
from jax import lax
from jax.experimental import pallas as pl
from jax.experimental.pallas import tpu as pltpu
from jax.sharding import Mesh, PartitionSpec as P

BF = jnp.bfloat16
F32 = jnp.float32
SWAP = [(0, 1), (1, 0)]
KDIM = 768

VM = pl.BlockSpec(memory_space=pltpu.VMEM)
SM = pl.BlockSpec(memory_space=pltpu.SMEM)
HBM = pl.BlockSpec(memory_space=pltpu.HBM)


def params():
    return pltpu.CompilerParams(vmem_limit_bytes=48 * 1024 * 1024)


def dot(a, b):
    return jnp.dot(a, b, preferred_element_type=F32)


def edge_masks(rows):
    column = lax.broadcasted_iota(jnp.int32, (rows, 256), 0) % 32
    return column != 0, column != 31


def forward_kernel(
    place_ref, valid_hbm, grad_hbm, join_hbm, maps_hbm, conv_hbm,
    out_ref, slope_ref, turned_ref,
    valid_ref, grad_ref, join_ref, maps_ref, conv_ref, rows_ref, sems,
):
    loads = [
        pltpu.make_async_copy(source, target, sems.at[i])
        for i, (source, target) in enumerate(
            (
                (valid_hbm, valid_ref),
                (grad_hbm, grad_ref),
                (join_hbm, join_ref),
                (maps_hbm, maps_ref),
                (conv_hbm, conv_ref),
            )
        )
    ]
    for load in loads:
        load.start()
    core, cam = place_ref[0], place_ref[1]
    loads[0].wait()
    valid = valid_ref[...].astype(F32)
    count = jnp.sum(valid, axis=1, keepdims=True)
    lane = lax.broadcasted_iota(jnp.int32, (2, 176), 1)
    weight = [jnp.sum(jnp.where(lane == cam * 11 + c, valid, 0.0), axis=1, keepdims=True) / count for c in range(11)]
    n = 11 * 32
    not_first, not_last = edge_masks(n)

    loads[1].wait()
    loads[2].wait()
    grad = grad_ref[...]
    for pos in range(4):
        part = lax.dot_general(
            grad, join_ref[256 * pos : 256 * pos + 256, :], (((1,), (1,)), ((), ())), preferred_element_type=F32
        )
        for j in range(2):
            rows_ref[4 * j + pos : 4 * j + pos + 1, :] = part[j : j + 1]
    out_ref[:, 0:8, :] = jnp.broadcast_to(rows_ref[0:8, :].astype(BF)[None], (16, 8, 256))

    loads[3].wait()
    loads[4].wait()
    for f in range(2):
        at = f * 11
        top = maps_ref[at : at + 11, 0:32, :].reshape(n, 256)
        low = maps_ref[at : at + 11, 32:64, :].reshape(n, 256)
        for r in range(2):
            taps = [
                dot(top, conv_ref[(1 - r) * 3 + dx]) + dot(low, conv_ref[(2 - r) * 3 + dx])
                for dx in range(3)
            ]
            pre = taps[1]
            pre = pre + jnp.where(not_first, pltpu.roll(taps[0], 1, 0), 0.0)
            pre = pre + jnp.where(not_last, pltpu.roll(taps[2], n - 1, 0), 0.0)
            sigma = jax.nn.sigmoid(pre)
            feature = pre * sigma
            slope = sigma * (1.0 + pre * (1.0 - sigma))
            pooled = jnp.zeros((32, 256), F32)
            for c in range(11):
                scale = weight[c][f : f + 1]
                rows = slice(32 * c, 32 * c + 32)
                pooled = pooled + feature[rows] * scale
                slope_ref[at + c, 32 * r : 32 * r + 32, :] = slope[rows] * scale
            for k in range(8):
                start = 8 * (8 * r + k) + 4 * f
                rows_ref[start : start + 4, :] = pooled[4 * k : 4 * k + 4]
    out_ref[:, 8:16, :] = rows_ref[...].reshape(16, 8, 256).astype(BF)

    m = 22 * 32
    keep_first, keep_last = edge_masks(m)
    for r in range(2):
        rows = maps_ref[:, 32 * r : 32 * r + 32, :].reshape(m, 256).astype(F32)
        for dx in range(3):
            if dx == 0:
                shifted = jnp.where(keep_first, pltpu.roll(rows, 1, 0), 0.0)
            elif dx == 1:
                shifted = rows
            else:
                shifted = jnp.where(keep_last, pltpu.roll(rows, m - 1, 0), 0.0)
            shifted = jnp.concatenate([shifted, jnp.zeros((KDIM - m, 256), F32)], 0)
            turned = shifted.T.astype(BF)
            for half in range(2):
                slot = core if half == 0 else 1 - core
                start = pl.multiple_of(slot * 384 + dx * 128, 128)
                turned_ref[r, pl.ds(start, 128), :] = turned[128 * half : 128 * half + 128]


def backward_kernel(grad_ref, slope_ref, turned_ref, mine_ref, send_ref, grads):
    for k in range(16):
        block = grad_ref[k, 0:8, :].astype(F32)
        for f in range(2):
            grads[f, 4 * k : 4 * k + 4, :] = block[4 * f : 4 * f + 4]
    pre = []
    for r in range(2):
        parts = []
        for f in range(2):
            rows = grads[f, 32 * r : 32 * r + 32, :]
            slope = slope_ref[11 * f : 11 * f + 11, 32 * r : 32 * r + 32, :]
            parts.append((slope * rows[None]).reshape(352, 256).astype(BF))
        parts.append(jnp.zeros((KDIM - 704, 256), BF))
        pre.append(jnp.concatenate(parts, 0))

    def put(dy, value):
        for slot, ref in enumerate((mine_ref, send_ref)):
            for dx in range(3):
                for h in range(2):
                    s = (dy * 3 + dx) * 2 + h
                    ref[128 * s : 128 * s + 128, :] = value[
                        slot * 384 + dx * 128 : slot * 384 + dx * 128 + 128, 128 * h : 128 * h + 128
                    ].astype(ref.dtype)

    put(0, dot(turned_ref[0], pre[1]))
    put(1, dot(turned_ref[0], pre[0]) + dot(turned_ref[1], pre[1]))
    put(2, dot(turned_ref[1], pre[0]))


def join_kernel(got_ref, join_ref, joined_ref, latent_ref):
    pooled = jnp.sum(got_ref[:, 8:16, :].astype(F32), axis=0)
    joined = pooled.astype(BF)
    joined_ref[...] = joined.astype(F32)
    parts = [dot(joined, join_ref[256 * pos : 256 * pos + 256, :]) for pos in range(4)]
    for j in range(2):
        latent_ref[j : j + 1, :] = sum(parts[pos][4 * j + pos : 4 * j + pos + 1] for pos in range(4))


def pack_kernel(place_ref, mine_ref, got_ref, joined_ref, latent_ref, grad_ref, out_ref, tail):
    total = (mine_ref[...] + got_ref[...].astype(F32)).astype(BF)
    out_ref[:, 0:144, :] = total.reshape(16, 144, 128)
    grad = grad_ref[...].astype(F32)
    tail[...] = jnp.zeros((16, 128), F32)
    for j in range(2):
        for h in range(2):
            tail[5 + 2 * j + h : 6 + 2 * j + h, :] = grad[j : j + 1, 128 * h : 128 * h + 128]
    for x in range(4):
        own = jnp.where(place_ref[2] == x, 1.0, 0.0)
        for j in range(2):
            for z in range(2):
                t = 4 * z + x
                row = 4 * j + t // 2
                lanes = slice(128 * (t % 2), 128 * (t % 2) + 128)
                tail[1 + 2 * j + z : 2 + 2 * j + z, :] = joined_ref[row : row + 1, lanes]
        for y in range(4):
            tail[0:1, :] = latent_ref[y // 2 : y // 2 + 1, 128 * (y % 2) : 128 * (y % 2) + 128] * own
            out_ref[4 * x + y, 144:160, :] = tail[...].astype(BF)


def middle_kernel(place_ref, got_ref, out_ref, ends):
    own_y = place_ref[3]
    conv = jnp.sum(got_ref[:, 0:144, :].astype(F32), axis=0)
    end = jnp.sum(got_ref[:, 144:160, :].astype(F32), axis=0)
    ends[...] = jnp.zeros((2, 32, 128), F32)
    for x in range(4):
        block = got_ref[4 * x + own_y, 144:160, :].astype(F32)
        for z in range(2):
            for j in range(2):
                ends[z, 1 + 2 * x + j : 2 + 2 * x + j, :] = block[1 + 2 * j + z : 2 + 2 * j + z]
            ends[z, 9 + 4 * x : 13 + 4 * x, :] = block[5:9]
    for z in range(2):
        ends[z, 0:1, :] = end[0:1]
    conv = conv.astype(BF)
    for z in range(8):
        out_ref[z, 0:144, :] = conv
        out_ref[z, 144:176, :] = ends[z % 2].astype(BF)


def finish_kernel(place_ref, got_ref, out_ref, rest_ref, rows_ref):
    own_high, own_low = place_ref[4], place_ref[5]
    conv = jnp.sum(got_ref[:, 0:144, :].astype(F32), axis=0).astype(BF)
    latent = jnp.zeros((8, 128), F32)
    for z in range(4):
        latent = latent + got_ref[2 * z + own_low, 144:176, :].astype(F32)[0:8]
    latent = latent.astype(BF)
    for k in range(16):
        out_ref[k, 0:144, :] = conv
        out_ref[k, 144:152, :] = latent
    for z in range(2):
        block = got_ref[2 * own_high + z, 144:176, :].astype(F32)
        rows_ref[8 * z : 8 * z + 8, 0:128] = block[1:9]
        for x in range(4):
            for j in range(2):
                for h in range(2):
                    row = 9 + 4 * x + 2 * j + h
                    at = 8 * z + 2 * x + j
                    rows_ref[at : at + 1, 128 + 128 * h : 256 + 128 * h] = block[row : row + 1]
    rest_ref[...] = rows_ref[...].astype(BF)


def spread_half(ref, conv_ref):
    for g in range(144):
        s, i, offset = g // 8, 16 * (g % 8), 16 * (g % 9)
        lanes = slice(128 * (s % 2), 128 * (s % 2) + 128)
        conv_ref[s // 2, i : i + 16, lanes] = ref[g // 9, offset : offset + 16, :].astype(F32)


def spread_own_kernel(place_ref, own_ref, conv_ref, latent_ref):
    spread_half(own_ref, conv_ref)
    for y in range(4):
        row = own_ref[4 * place_ref[2] + y, 144:152, :].astype(F32)[0:1]
        latent_ref[y // 2 : y // 2 + 1, 128 * (y % 2) : 128 * (y % 2) + 128] = row


def spread_other_kernel(place_ref, other_ref, begun_ref, conv_ref):
    spread_half(other_ref, conv_ref)


def spread(kernel, name, place, blocks, begun=None):
    own = begun is None
    whole = pl.BlockSpec((16, 152, 128), lambda i, at: (0, 0, 0))
    half = pl.BlockSpec((9, 128, 256), lambda i, at: (0, at[0] if own else 1 - at[0], 0))
    conv_shape = shape(9, 256, 256)
    return pl.pallas_call(
        kernel,
        out_shape=[conv_shape, shape(2, 256)] if own else [conv_shape],
        grid_spec=pltpu.PrefetchScalarGridSpec(
            num_scalar_prefetch=1,
            grid=(1,),
            in_specs=[whole] if own else [whole, HBM],
            out_specs=[half, pl.BlockSpec((2, 256), lambda i, at: (0, 0))] if own else [half],
        ),
        input_output_aliases={} if own else {2: 0},
        compiler_params=params(),
        cost_estimate=pl.CostEstimate(flops=1_000_000, bytes_accessed=2_000_000, transcendentals=0),
        name=name,
    )(place, blocks, *(() if own else (begun,)))


def shape(*dims, dtype=F32):
    return jax.ShapeDtypeStruct(dims, dtype)


def call(kernel, name, out_shape, in_specs, scratch=(), flops=1_000_000, moved=3_000_000):
    return pl.pallas_call(
        kernel,
        out_shape=out_shape,
        in_specs=in_specs,
        out_specs=[VM] * len(out_shape),
        scratch_shapes=scratch,
        compiler_params=params(),
        cost_estimate=pl.CostEstimate(flops=flops, bytes_accessed=moved, transcendentals=0),
        name=name,
    )


def in_hbm(array):
    return pltpu.with_memory_space_constraint(array, pltpu.HBM)


def on_device(view_maps, conv_weight, join_weight, valid_cams, latent_grad):
    names = ("c", ("zh", "y"), "x", "y", "zh", "zl")
    place = jnp.stack([lax.axis_index(name).astype(jnp.int32) for name in names])

    with jax.named_scope("forward"):
        shares, slope, turned = call(
            forward_kernel,
            "forward",
            [shape(16, 16, 256, dtype=BF), shape(22, 64, 256), shape(2, 768, KDIM, dtype=BF)],
            [SM, HBM, HBM, HBM, HBM, HBM],
            [
                pltpu.VMEM((2, 176), jnp.int32),
                pltpu.VMEM((2, 256), BF),
                pltpu.VMEM((1024, 256), BF),
                pltpu.VMEM((22, 64, 256), BF),
                pltpu.VMEM((9, 256, 256), BF),
                pltpu.VMEM((128, 256), F32),
                pltpu.SemaphoreType.DMA((5,)),
            ],
            flops=1_200_000_000,
        )(place, *map(in_hbm, (valid_cams, latent_grad, join_weight, view_maps.reshape(22, 64, 256), conv_weight)))
        cam_shares = lax.all_to_all(shares, ("zh", "y"), 0, 0)

    with jax.named_scope("backward"):
        mine, send = call(
            backward_kernel,
            "backward",
            [shape(2304, 128), shape(2304, 128, dtype=BF)],
            [VM, VM, VM],
            [pltpu.VMEM((2, 64, 256), F32)],
            flops=1_200_000_000,
        )(cam_shares, slope, turned)
        got = lax.ppermute(send, "c", SWAP)

    with jax.named_scope("join"):
        joined, latent_part = call(join_kernel, "join", [shape(8, 256), shape(2, 256)], [VM, VM])(
            cam_shares, join_weight
        )

    with jax.named_scope("conv_scatter"):
        (packed,) = call(
            pack_kernel,
            "pack",
            [shape(16, 160, 128, dtype=BF)],
            [SM, VM, VM, VM, VM, VM],
            [pltpu.VMEM((16, 128), F32)],
        )(place, mine, got, joined, latent_part, latent_grad)
        blocks = lax.all_to_all(packed, ("x", "y"), 0, 0)

    with jax.named_scope("conv_middle"):
        (middle,) = call(
            middle_kernel, "middle", [shape(8, 176, 128, dtype=BF)], [SM, VM], [pltpu.VMEM((2, 32, 128), F32)]
        )(place, blocks)
        lines = lax.all_to_all(middle, ("zh", "zl"), 0, 0)

    with jax.named_scope("conv_gather"):
        summed, rest = call(
            finish_kernel,
            "finish",
            [shape(16, 152, 128, dtype=BF), shape(16, 384, dtype=BF)],
            [SM, VM],
            [pltpu.VMEM((16, 384), F32)],
        )(place, lines)
        own = lax.all_to_all(summed, ("x", "y"), 0, 0)
        other = lax.ppermute(own, "c", SWAP)
        begun, latent = spread(spread_own_kernel, "spread_own", place, own)

    with jax.named_scope("join_grad"):
        rest_other = lax.ppermute(rest, "c", SWAP)
        both = jnp.concatenate([rest, rest_other], 0)
        rows = lax.dynamic_slice_in_dim(both, place[0] * 64, 64, 1)
        join_grad = lax.dot_general(rows, both[:, 128:], (((0,), (0,)), ((), ())), preferred_element_type=F32)

    with jax.named_scope("conv_end"):
        (conv_grad,) = spread(spread_other_kernel, "spread_other", place, other, begun)
    return (latent, conv_grad, join_grad)


def solution(mesh):
    fine = Mesh(mesh.devices.reshape(2, 4, 2, 4, 4), ("zl", "x", "c", "zh", "y"))
    frame, cam = ("zl", "x", "c"), ("zh", "y")
    in_specs = (
        P(frame, cam, None, None, None),
        P(),
        P(cam, None),
        P(frame, None),
        P(frame, None),
    )
    out_specs = (P(frame, None), P(), P(cam + frame, None))
    return jax.shard_map(on_device, mesh=fine, in_specs=in_specs, out_specs=out_specs, check_vma=False)
```

```python
import functools

import jax
import jax.numpy as jnp
from jax import lax
from jax.experimental import pallas as pl
from jax.experimental.pallas import tpu as pltpu
from jax.sharding import Mesh, PartitionSpec as P

BF = jnp.bfloat16
F32 = jnp.float32
SWAP = [(0, 1), (1, 0)]
KDIM = 768

VM = pl.BlockSpec(memory_space=pltpu.VMEM)
SM = pl.BlockSpec(memory_space=pltpu.SMEM)
HBM = pl.BlockSpec(memory_space=pltpu.HBM)


def params():
    return pltpu.CompilerParams(vmem_limit_bytes=48 * 1024 * 1024)


def dot(a, b):
    return jnp.dot(a, b, preferred_element_type=F32)


def edge_masks(rows):
    column = lax.broadcasted_iota(jnp.int32, (rows, 256), 0) % 32
    return column != 0, column != 31


def forward_kernel(
    place_ref, valid_hbm, grad_hbm, join_hbm, maps_hbm, conv_hbm,
    out_ref, slope_ref, turned_ref,
    valid_ref, grad_ref, join_ref, maps_ref, conv_ref, rows_ref, sems,
):
    loads = [
        pltpu.make_async_copy(source, target, sems.at[i])
        for i, (source, target) in enumerate(
            (
                (valid_hbm, valid_ref),
                (grad_hbm, grad_ref),
                (join_hbm, join_ref),
                (maps_hbm, maps_ref),
                (conv_hbm, conv_ref),
            )
        )
    ]
    for load in loads:
        load.start()
    core, cam = place_ref[0], place_ref[1]
    loads[0].wait()
    valid = valid_ref[...].astype(F32)
    count = jnp.sum(valid, axis=1, keepdims=True)
    lane = lax.broadcasted_iota(jnp.int32, (2, 176), 1)
    weight = [jnp.sum(jnp.where(lane == cam * 11 + c, valid, 0.0), axis=1, keepdims=True) / count for c in range(11)]
    n = 11 * 32
    not_first, not_last = edge_masks(n)

    loads[1].wait()
    loads[2].wait()
    grad = grad_ref[...]
    for pos in range(4):
        part = lax.dot_general(
            grad, join_ref[256 * pos : 256 * pos + 256, :], (((1,), (1,)), ((), ())), preferred_element_type=F32
        )
        for j in range(2):
            rows_ref[4 * j + pos : 4 * j + pos + 1, :] = part[j : j + 1]
    out_ref[:, 0:8, :] = jnp.broadcast_to(rows_ref[0:8, :].astype(BF)[None], (16, 8, 256))

    loads[3].wait()
    loads[4].wait()
    for f in range(2):
        at = f * 11
        top = maps_ref[at : at + 11, 0:32, :].reshape(n, 256)
        low = maps_ref[at : at + 11, 32:64, :].reshape(n, 256)
        for r in range(2):
            taps = [
                dot(top, conv_ref[(1 - r) * 3 + dx]) + dot(low, conv_ref[(2 - r) * 3 + dx])
                for dx in range(3)
            ]
            pre = taps[1]
            pre = pre + jnp.where(not_first, pltpu.roll(taps[0], 1, 0), 0.0)
            pre = pre + jnp.where(not_last, pltpu.roll(taps[2], n - 1, 0), 0.0)
            sigma = jax.nn.sigmoid(pre)
            feature = pre * sigma
            slope = sigma * (1.0 + pre * (1.0 - sigma))
            pooled = jnp.zeros((32, 256), F32)
            for c in range(11):
                scale = weight[c][f : f + 1]
                rows = slice(32 * c, 32 * c + 32)
                pooled = pooled + feature[rows] * scale
                slope_ref[at + c, 32 * r : 32 * r + 32, :] = slope[rows] * scale
            for k in range(8):
                start = 8 * (8 * r + k) + 4 * f
                rows_ref[start : start + 4, :] = pooled[4 * k : 4 * k + 4]
    out_ref[:, 8:16, :] = rows_ref[...].reshape(16, 8, 256).astype(BF)

    m = 22 * 32
    keep_first, keep_last = edge_masks(m)
    for r in range(2):
        rows = maps_ref[:, 32 * r : 32 * r + 32, :].reshape(m, 256).astype(F32)
        for dx in range(3):
            if dx == 0:
                shifted = jnp.where(keep_first, pltpu.roll(rows, 1, 0), 0.0)
            elif dx == 1:
                shifted = rows
            else:
                shifted = jnp.where(keep_last, pltpu.roll(rows, m - 1, 0), 0.0)
            shifted = jnp.concatenate([shifted, jnp.zeros((KDIM - m, 256), F32)], 0)
            turned = shifted.T.astype(BF)
            for half in range(2):
                slot = core if half == 0 else 1 - core
                start = pl.multiple_of(slot * 384 + dx * 128, 128)
                turned_ref[r, pl.ds(start, 128), :] = turned[128 * half : 128 * half + 128]


def send_kernel(grad_ref, slope_ref, turned_ref, pre_ref, send_ref, grads):
    for k in range(16):
        block = grad_ref[k, 0:8, :].astype(F32)
        for f in range(2):
            grads[f, 4 * k : 4 * k + 4, :] = block[4 * f : 4 * f + 4]
    pre = []
    for r in range(2):
        parts = []
        for f in range(2):
            rows = grads[f, 32 * r : 32 * r + 32, :]
            slope = slope_ref[11 * f : 11 * f + 11, 32 * r : 32 * r + 32, :]
            parts.append((slope * rows[None]).reshape(352, 256).astype(BF))
        parts.append(jnp.zeros((KDIM - 704, 256), BF))
        pre.append(jnp.concatenate(parts, 0))

    for r in range(2):
        pre_ref[r] = pre[r]
    half_taps(turned_ref, pre_ref, 1, send_ref)


def half_taps(turned_ref, pre_ref, slot, out_ref):
    part = slice(384 * slot, 384 * slot + 384)
    top, low = turned_ref[0, part], turned_ref[1, part]
    for dy in range(3):
        if dy == 0:
            value = dot(top, pre_ref[1])
        elif dy == 1:
            value = dot(top, pre_ref[0]) + dot(low, pre_ref[1])
        else:
            value = dot(low, pre_ref[0])
        for dx in range(3):
            for h in range(2):
                s = (dy * 3 + dx) * 2 + h
                out_ref[128 * s : 128 * s + 128, :] = value[
                    128 * dx : 128 * dx + 128, 128 * h : 128 * h + 128
                ].astype(out_ref.dtype)


def mine_kernel(turned_ref, pre_ref, got_ref, join_ref, mine_ref, joined_ref, latent_ref):
    half_taps(turned_ref, pre_ref, 0, mine_ref)
    pooled = jnp.sum(got_ref[:, 8:16, :].astype(F32), axis=0)
    joined = pooled.astype(BF)
    joined_ref[...] = joined.astype(F32)
    parts = [dot(joined, join_ref[256 * pos : 256 * pos + 256, :]) for pos in range(4)]
    for j in range(2):
        latent_ref[j : j + 1, :] = sum(parts[pos][4 * j + pos : 4 * j + pos + 1] for pos in range(4))


def pack_kernel(place_ref, mine_ref, got_ref, joined_ref, latent_ref, grad_ref, out_ref, tail):
    total = (mine_ref[...] + got_ref[...].astype(F32)).astype(BF)
    out_ref[:, 0:144, :] = total.reshape(16, 144, 128)
    grad = grad_ref[...].astype(F32)
    tail[...] = jnp.zeros((16, 128), F32)
    for j in range(2):
        for h in range(2):
            tail[5 + 2 * j + h : 6 + 2 * j + h, :] = grad[j : j + 1, 128 * h : 128 * h + 128]
    for x in range(4):
        own = jnp.where(place_ref[2] == x, 1.0, 0.0)
        for j in range(2):
            for z in range(2):
                t = 4 * z + x
                row = 4 * j + t // 2
                lanes = slice(128 * (t % 2), 128 * (t % 2) + 128)
                tail[1 + 2 * j + z : 2 + 2 * j + z, :] = joined_ref[row : row + 1, lanes]
        for y in range(4):
            tail[0:1, :] = latent_ref[y // 2 : y // 2 + 1, 128 * (y % 2) : 128 * (y % 2) + 128] * own
            out_ref[4 * x + y, 144:160, :] = tail[...].astype(BF)


def middle_kernel(place_ref, got_ref, out_ref, ends):
    own_y = place_ref[3]
    conv = jnp.sum(got_ref[:, 0:144, :].astype(F32), axis=0)
    end = jnp.sum(got_ref[:, 144:160, :].astype(F32), axis=0)
    ends[...] = jnp.zeros((2, 32, 128), F32)
    for x in range(4):
        block = got_ref[4 * x + own_y, 144:160, :].astype(F32)
        for z in range(2):
            for j in range(2):
                ends[z, 1 + 2 * x + j : 2 + 2 * x + j, :] = block[1 + 2 * j + z : 2 + 2 * j + z]
            ends[z, 9 + 4 * x : 13 + 4 * x, :] = block[5:9]
    for z in range(2):
        ends[z, 0:1, :] = end[0:1]
    conv = conv.astype(BF)
    for z in range(8):
        out_ref[z, 0:144, :] = conv
        out_ref[z, 144:176, :] = ends[z % 2].astype(BF)


def finish_kernel(place_ref, got_ref, out_ref, rest_ref, rows_ref):
    own_high, own_low = place_ref[4], place_ref[5]
    conv = jnp.sum(got_ref[:, 0:144, :].astype(F32), axis=0).astype(BF)
    latent = jnp.zeros((8, 128), F32)
    for z in range(4):
        latent = latent + got_ref[2 * z + own_low, 144:176, :].astype(F32)[0:8]
    latent = latent.astype(BF)
    for k in range(16):
        out_ref[k, 0:144, :] = conv
        out_ref[k, 144:152, :] = latent
    for z in range(2):
        block = got_ref[2 * own_high + z, 144:176, :].astype(F32)
        rows_ref[8 * z : 8 * z + 8, 0:128] = block[1:9]
        for x in range(4):
            for j in range(2):
                for h in range(2):
                    row = 9 + 4 * x + 2 * j + h
                    at = 8 * z + 2 * x + j
                    rows_ref[at : at + 1, 128 + 128 * h : 256 + 128 * h] = block[row : row + 1]
    rest_ref[...] = rows_ref[...].astype(BF)


def spread_half(ref, half, conv_hbm, slabs, sems):
    copies = []
    for t in range(9):
        for g in range(16 * t, 16 * t + 16):
            s, i, offset = g // 8, 16 * (g % 8), 16 * (g % 9)
            lanes = slice(128 * (s % 2), 128 * (s % 2) + 128)
            slabs[t, i : i + 16, lanes] = ref[g // 9, offset : offset + 16, :].astype(F32)
        rows = pl.ds(pl.multiple_of(128 * half, 128), 128)
        copies.append(pltpu.make_async_copy(slabs.at[t], conv_hbm.at[t, rows], sems.at[t]))
        copies[t].start()
    return copies


def spread_own_kernel(place_ref, own_ref, conv_hbm, latent_ref, slabs, sems):
    copies = spread_half(own_ref, place_ref[0], conv_hbm, slabs, sems)
    for y in range(4):
        row = own_ref[4 * place_ref[2] + y, 144:152, :].astype(F32)[0:1]
        latent_ref[y // 2 : y // 2 + 1, 128 * (y % 2) : 128 * (y % 2) + 128] = row
    for copy in copies:
        copy.wait()


def spread_other_kernel(place_ref, other_ref, rest_ref, rest_other_ref, begun_hbm, conv_hbm, join_ref, slabs, sems):
    core = place_ref[0]
    copies = spread_half(other_ref, 1 - core, conv_hbm, slabs, sems)
    total = jnp.zeros((64, 256), F32)
    for ref in (rest_ref, rest_other_ref):
        rows = ref[...]
        joined = jnp.where(core == 0, rows[:, 0:64], rows[:, 64:128])
        total = total + lax.dot_general(joined, rows[:, 128:384], (((0,), (0,)), ((), ())), preferred_element_type=F32)
    join_ref[...] = total
    for copy in copies:
        copy.wait()


def spread(kernel, name, out_shape, in_specs, aliases):
    return pl.pallas_call(
        kernel,
        out_shape=out_shape,
        in_specs=in_specs,
        out_specs=[HBM, VM],
        scratch_shapes=[pltpu.VMEM((9, 128, 256), F32), pltpu.SemaphoreType.DMA((9,))],
        input_output_aliases=aliases,
        compiler_params=params(),
        cost_estimate=pl.CostEstimate(flops=1_000_000, bytes_accessed=2_000_000, transcendentals=0),
        name=name,
    )


def shape(*dims, dtype=F32):
    return jax.ShapeDtypeStruct(dims, dtype)


def call(kernel, name, out_shape, in_specs, scratch=(), flops=1_000_000, moved=3_000_000):
    return pl.pallas_call(
        kernel,
        out_shape=out_shape,
        in_specs=in_specs,
        out_specs=[VM] * len(out_shape),
        scratch_shapes=scratch,
        compiler_params=params(),
        cost_estimate=pl.CostEstimate(flops=flops, bytes_accessed=moved, transcendentals=0),
        name=name,
    )


def in_hbm(array):
    return pltpu.with_memory_space_constraint(array, pltpu.HBM)


def on_device(view_maps, conv_weight, join_weight, valid_cams, latent_grad):
    names = ("c", ("zh", "y"), "x", "y", "zh", "zl")
    place = jnp.stack([lax.axis_index(name).astype(jnp.int32) for name in names])

    with jax.named_scope("forward"):
        shares, slope, turned = call(
            forward_kernel,
            "forward",
            [shape(16, 16, 256, dtype=BF), shape(22, 64, 256), shape(2, 768, KDIM, dtype=BF)],
            [SM, HBM, HBM, HBM, HBM, HBM],
            [
                pltpu.VMEM((2, 176), jnp.int32),
                pltpu.VMEM((2, 256), BF),
                pltpu.VMEM((1024, 256), BF),
                pltpu.VMEM((22, 64, 256), BF),
                pltpu.VMEM((9, 256, 256), BF),
                pltpu.VMEM((128, 256), F32),
                pltpu.SemaphoreType.DMA((5,)),
            ],
            flops=1_200_000_000,
        )(place, *map(in_hbm, (valid_cams, latent_grad, join_weight, view_maps.reshape(22, 64, 256), conv_weight)))
        cam_shares = lax.all_to_all(shares, ("zh", "y"), 0, 0)

    with jax.named_scope("backward"):
        pre_grad, send = call(
            send_kernel,
            "backward_send",
            [shape(2, KDIM, 256, dtype=BF), shape(2304, 128, dtype=BF)],
            [VM, VM, VM],
            [pltpu.VMEM((2, 64, 256), F32)],
            flops=600_000_000,
        )(cam_shares, slope, turned)
        got = lax.ppermute(send, "c", SWAP)
        mine, joined, latent_part = call(
            mine_kernel,
            "backward_mine",
            [shape(2304, 128), shape(8, 256), shape(2, 256)],
            [VM, VM, VM, VM],
            flops=600_000_000,
        )(turned, pre_grad, cam_shares, join_weight)

    with jax.named_scope("conv_scatter"):
        (packed,) = call(
            pack_kernel,
            "pack",
            [shape(16, 160, 128, dtype=BF)],
            [SM, VM, VM, VM, VM, VM],
            [pltpu.VMEM((16, 128), F32)],
        )(place, mine, got, joined, latent_part, latent_grad)
        blocks = lax.all_to_all(packed, ("x", "y"), 0, 0)

    with jax.named_scope("conv_middle"):
        (middle,) = call(
            middle_kernel, "middle", [shape(8, 176, 128, dtype=BF)], [SM, VM], [pltpu.VMEM((2, 32, 128), F32)]
        )(place, blocks)
        lines = lax.all_to_all(middle, ("zh", "zl"), 0, 0)

    with jax.named_scope("conv_gather"):
        summed, rest = call(
            finish_kernel,
            "finish",
            [shape(16, 152, 128, dtype=BF), shape(16, 384, dtype=BF)],
            [SM, VM],
            [pltpu.VMEM((16, 384), F32)],
        )(place, lines)
        own = lax.all_to_all(summed, ("x", "y"), 0, 0)
        other = lax.ppermute(own, "c", SWAP)
        begun, latent = spread(
            spread_own_kernel, "spread_own", [shape(9, 256, 256), shape(2, 256)], [SM, VM], {}
        )(place, own)

    with jax.named_scope("end"):
        rest_other = lax.ppermute(rest, "c", SWAP)
        conv_grad, join_grad = spread(
            spread_other_kernel, "spread_other", [shape(9, 256, 256), shape(64, 256)], [SM, VM, VM, VM, HBM], {4: 0}
        )(place, other, rest, rest_other, begun)
    return (latent, conv_grad, join_grad)


def solution(mesh):
    fine = Mesh(mesh.devices.reshape(2, 4, 2, 4, 4), ("zl", "x", "c", "zh", "y"))
    frame, cam = ("zl", "x", "c"), ("zh", "y")
    in_specs = (
        P(frame, cam, None, None, None),
        P(),
        P(cam, None),
        P(frame, None),
        P(frame, None),
    )
    out_specs = (P(frame, None), P(), P(cam + frame, None))
    return jax.shard_map(on_device, mesh=fine, in_specs=in_specs, out_specs=out_specs, check_vma=False)
```

```python
import functools

import jax
import jax.numpy as jnp
from jax import lax
from jax.experimental import pallas as pl
from jax.experimental.pallas import tpu as pltpu
from jax.sharding import Mesh, PartitionSpec as P

BF = jnp.bfloat16
F32 = jnp.float32
SWAP = [(0, 1), (1, 0)]
BLOCK = ("zl", "x", "y")
KDIM = 768

VM = pl.BlockSpec(memory_space=pltpu.VMEM)
SM = pl.BlockSpec(memory_space=pltpu.SMEM)
HBM = pl.BlockSpec(memory_space=pltpu.HBM)


def params():
    return pltpu.CompilerParams(vmem_limit_bytes=48 * 1024 * 1024)


def dot(a, b):
    return jnp.dot(a, b, preferred_element_type=F32)


def edge_masks(rows):
    column = lax.broadcasted_iota(jnp.int32, (rows, 256), 0) % 32
    return column != 0, column != 31


def forward_kernel(
    place_ref, valid_hbm, grad_hbm, join_hbm, maps_hbm, conv_hbm,
    out_ref, slope_ref, turned_ref,
    valid_ref, grad_ref, join_ref, maps_ref, conv_ref, rows_ref, sems,
):
    loads = [
        pltpu.make_async_copy(source, target, sems.at[i])
        for i, (source, target) in enumerate(
            (
                (valid_hbm, valid_ref),
                (grad_hbm, grad_ref),
                (join_hbm, join_ref),
                (maps_hbm, maps_ref),
                (conv_hbm, conv_ref),
            )
        )
    ]
    for load in loads:
        load.start()
    core, cam = place_ref[0], place_ref[1]
    loads[0].wait()
    valid = valid_ref[...].astype(F32)
    count = jnp.sum(valid, axis=1, keepdims=True)
    lane = lax.broadcasted_iota(jnp.int32, (2, 176), 1)
    weight = [jnp.sum(jnp.where(lane == cam * 11 + c, valid, 0.0), axis=1, keepdims=True) / count for c in range(11)]
    n = 11 * 32
    not_first, not_last = edge_masks(n)

    loads[1].wait()
    loads[2].wait()
    grad = grad_ref[...]
    for pos in range(4):
        part = lax.dot_general(
            grad, join_ref[256 * pos : 256 * pos + 256, :], (((1,), (1,)), ((), ())), preferred_element_type=F32
        )
        for j in range(2):
            rows_ref[4 * j + pos : 4 * j + pos + 1, :] = part[j : j + 1]
    out_ref[:, 0:8, :] = jnp.broadcast_to(rows_ref[0:8, :].astype(BF)[None], (16, 8, 256))

    loads[3].wait()
    loads[4].wait()
    for f in range(2):
        at = f * 11
        top = maps_ref[at : at + 11, 0:32, :].reshape(n, 256)
        low = maps_ref[at : at + 11, 32:64, :].reshape(n, 256)
        for r in range(2):
            taps = [
                dot(top, conv_ref[(1 - r) * 3 + dx]) + dot(low, conv_ref[(2 - r) * 3 + dx])
                for dx in range(3)
            ]
            pre = taps[1]
            pre = pre + jnp.where(not_first, pltpu.roll(taps[0], 1, 0), 0.0)
            pre = pre + jnp.where(not_last, pltpu.roll(taps[2], n - 1, 0), 0.0)
            sigma = jax.nn.sigmoid(pre)
            feature = pre * sigma
            slope = sigma * (1.0 + pre * (1.0 - sigma))
            pooled = jnp.zeros((32, 256), F32)
            for c in range(11):
                scale = weight[c][f : f + 1]
                rows = slice(32 * c, 32 * c + 32)
                pooled = pooled + feature[rows] * scale
                slope_ref[at + c, 32 * r : 32 * r + 32, :] = slope[rows] * scale
            for k in range(8):
                start = 8 * (8 * r + k) + 4 * f
                rows_ref[start : start + 4, :] = pooled[4 * k : 4 * k + 4]
    out_ref[:, 8:16, :] = rows_ref[...].reshape(16, 8, 256).astype(BF)

    m = 22 * 32
    keep_first, keep_last = edge_masks(m)
    for r in range(2):
        rows = maps_ref[:, 32 * r : 32 * r + 32, :].reshape(m, 256).astype(F32)
        for dx in range(3):
            if dx == 0:
                shifted = jnp.where(keep_first, pltpu.roll(rows, 1, 0), 0.0)
            elif dx == 1:
                shifted = rows
            else:
                shifted = jnp.where(keep_last, pltpu.roll(rows, m - 1, 0), 0.0)
            shifted = jnp.concatenate([shifted, jnp.zeros((KDIM - m, 256), F32)], 0)
            turned = shifted.T.astype(BF)
            for half in range(2):
                slot = core if half == 0 else 1 - core
                start = pl.multiple_of(slot * 384 + dx * 128, 128)
                turned_ref[r, pl.ds(start, 128), :] = turned[128 * half : 128 * half + 128]


def send_kernel(grad_ref, slope_ref, turned_ref, pre_ref, send_ref, grads):
    for k in range(16):
        block = grad_ref[k, 0:8, :].astype(F32)
        for f in range(2):
            grads[f, 4 * k : 4 * k + 4, :] = block[4 * f : 4 * f + 4]
    pre = []
    for r in range(2):
        parts = []
        for f in range(2):
            rows = grads[f, 32 * r : 32 * r + 32, :]
            slope = slope_ref[11 * f : 11 * f + 11, 32 * r : 32 * r + 32, :]
            parts.append((slope * rows[None]).reshape(352, 256).astype(BF))
        parts.append(jnp.zeros((KDIM - 704, 256), BF))
        pre.append(jnp.concatenate(parts, 0))

    for r in range(2):
        pre_ref[r] = pre[r]
    half_taps(turned_ref, pre_ref, 1, send_ref)


def half_taps(turned_ref, pre_ref, slot, out_ref):
    part = slice(384 * slot, 384 * slot + 384)
    top, low = turned_ref[0, part], turned_ref[1, part]
    for dy in range(3):
        if dy == 0:
            value = dot(top, pre_ref[1])
        elif dy == 1:
            value = dot(top, pre_ref[0]) + dot(low, pre_ref[1])
        else:
            value = dot(low, pre_ref[0])
        for dx in range(3):
            for h in range(2):
                s = (dy * 3 + dx) * 2 + h
                out_ref[128 * s : 128 * s + 128, :] = value[
                    128 * dx : 128 * dx + 128, 128 * h : 128 * h + 128
                ].astype(out_ref.dtype)


def mine_kernel(turned_ref, pre_ref, got_ref, join_ref, mine_ref, joined_ref, latent_ref):
    half_taps(turned_ref, pre_ref, 0, mine_ref)
    pooled = jnp.sum(got_ref[:, 8:16, :].astype(F32), axis=0)
    joined = pooled.astype(BF)
    joined_ref[...] = joined.astype(F32)
    parts = [dot(joined, join_ref[256 * pos : 256 * pos + 256, :]) for pos in range(4)]
    for j in range(2):
        latent_ref[j : j + 1, :] = sum(parts[pos][4 * j + pos : 4 * j + pos + 1] for pos in range(4))


def pack_kernel(place_ref, mine_ref, got_ref, joined_ref, latent_ref, grad_ref, out_ref, last):
    head = (mine_ref[0:2048] + got_ref[0:2048].astype(F32)).astype(BF)
    out_ref[:, 0:64, :] = head.reshape(32, 64, 128)
    foot = mine_ref[2048:2304] + got_ref[2048:2304].astype(F32)
    grad = grad_ref[...].astype(F32)
    last[...] = jnp.zeros((16, 128), F32)
    for j in range(2):
        for h in range(2):
            last[11 + 2 * j + h : 12 + 2 * j + h, :] = grad[j : j + 1, 128 * h : 128 * h + 128]
    for z in range(2):
        for x in range(4):
            t = 4 * z + x
            lanes = slice(128 * (t % 2), 128 * (t % 2) + 128)
            for j in range(2):
                row = 4 * j + t // 2
                last[9 + j : 10 + j, :] = joined_ref[row : row + 1, lanes]
            own = jnp.where(jnp.logical_and(place_ref[2] == x, place_ref[4] == z), 1.0, 0.0)
            for y in range(4):
                b = 4 * t + y
                last[0:8, :] = foot[8 * b : 8 * b + 8]
                last[8:9, :] = latent_ref[y // 2 : y // 2 + 1, 128 * (y % 2) : 128 * (y % 2) + 128] * own
                out_ref[b, 64:80, :] = last[...].astype(BF)


def middle_kernel(place_ref, got_ref, out_ref, rest_ref, rows_ref):
    head = jnp.sum(got_ref[:, 0:64, :].astype(F32), axis=0).astype(BF)
    foot = jnp.sum(got_ref[:, 64:80, :].astype(F32), axis=0).astype(BF)
    for z in range(4):
        out_ref[z, 0:64, :] = head
        out_ref[z, 64:80, :] = foot
    for k in range(8):
        last = got_ref[4 * k + place_ref[3], 64:80, :].astype(F32)
        for j in range(2):
            at = slice(2 * k + j, 2 * k + j + 1)
            rows_ref[at, 0:128] = last[9 + j : 10 + j]
            for h in range(2):
                row = 11 + 2 * j + h
                rows_ref[at, 128 + 128 * h : 256 + 128 * h] = last[row : row + 1]
    rest_ref[...] = rows_ref[...].astype(BF)


def finish_kernel(got_ref, out_ref):
    total = jnp.sum(got_ref[...].astype(F32), axis=0).astype(BF)
    for b in range(32):
        out_ref[b] = total


def spread_half(ref, half, conv_hbm, slabs, sem):
    for b in range(32):
        s, i = b // 2, 64 * (b % 2)
        lanes = slice(128 * (s % 2), 128 * (s % 2) + 128)
        slabs[s // 2, i : i + 64, lanes] = ref[b, 0:64, :].astype(F32)
        s, i = b // 16, 8 * (b % 16)
        slabs[8, i : i + 8, 128 * s : 128 * s + 128] = ref[b, 64:80, :].astype(F32)[0:8]
    rows = pl.ds(pl.multiple_of(128 * half, 128), 128)
    copy = pltpu.make_async_copy(slabs, conv_hbm.at[:, rows], sem)
    copy.start()
    return copy


def spread_own_kernel(place_ref, own_ref, conv_hbm, latent_ref, slabs, sem):
    copy = spread_half(own_ref, place_ref[0], conv_hbm, slabs, sem)
    first = 16 * place_ref[4] + 4 * place_ref[2]
    for y in range(4):
        row = own_ref[first + y, 64:80, :].astype(F32)[8:9]
        latent_ref[y // 2 : y // 2 + 1, 128 * (y % 2) : 128 * (y % 2) + 128] = row
    copy.wait()


def spread_other_kernel(place_ref, other_ref, rest_ref, rest_other_ref, begun_hbm, conv_hbm, join_ref, slabs, sem):
    core = place_ref[0]
    copy = spread_half(other_ref, 1 - core, conv_hbm, slabs, sem)
    total = jnp.zeros((64, 256), F32)
    for ref in (rest_ref, rest_other_ref):
        rows = ref[...]
        joined = jnp.where(core == 0, rows[:, 0:64], rows[:, 64:128])
        total = total + lax.dot_general(joined, rows[:, 128:384], (((0,), (0,)), ((), ())), preferred_element_type=F32)
    join_ref[...] = total
    copy.wait()


def spread(kernel, name, out_shape, in_specs, aliases):
    return pl.pallas_call(
        kernel,
        out_shape=out_shape,
        in_specs=in_specs,
        out_specs=[HBM, VM],
        scratch_shapes=[pltpu.VMEM((9, 128, 256), F32), pltpu.SemaphoreType.DMA],
        input_output_aliases=aliases,
        compiler_params=params(),
        cost_estimate=pl.CostEstimate(flops=1_000_000, bytes_accessed=2_000_000, transcendentals=0),
        name=name,
    )


def shape(*dims, dtype=F32):
    return jax.ShapeDtypeStruct(dims, dtype)


def call(kernel, name, out_shape, in_specs, scratch=(), flops=1_000_000, moved=3_000_000):
    return pl.pallas_call(
        kernel,
        out_shape=out_shape,
        in_specs=in_specs,
        out_specs=[VM] * len(out_shape),
        scratch_shapes=scratch,
        compiler_params=params(),
        cost_estimate=pl.CostEstimate(flops=flops, bytes_accessed=moved, transcendentals=0),
        name=name,
    )


def in_hbm(array):
    return pltpu.with_memory_space_constraint(array, pltpu.HBM)


def on_device(view_maps, conv_weight, join_weight, valid_cams, latent_grad):
    names = ("c", ("zh", "y"), "x", "y", "zl")
    place = jnp.stack([lax.axis_index(name).astype(jnp.int32) for name in names])

    with jax.named_scope("forward"):
        shares, slope, turned = call(
            forward_kernel,
            "forward",
            [shape(16, 16, 256, dtype=BF), shape(22, 64, 256), shape(2, 768, KDIM, dtype=BF)],
            [SM, HBM, HBM, HBM, HBM, HBM],
            [
                pltpu.VMEM((2, 176), jnp.int32),
                pltpu.VMEM((2, 256), BF),
                pltpu.VMEM((1024, 256), BF),
                pltpu.VMEM((22, 64, 256), BF),
                pltpu.VMEM((9, 256, 256), BF),
                pltpu.VMEM((128, 256), F32),
                pltpu.SemaphoreType.DMA((5,)),
            ],
            flops=1_200_000_000,
        )(place, *map(in_hbm, (valid_cams, latent_grad, join_weight, view_maps.reshape(22, 64, 256), conv_weight)))
        cam_shares = lax.all_to_all(shares, ("zh", "y"), 0, 0)

    with jax.named_scope("backward"):
        pre_grad, send = call(
            send_kernel,
            "backward_send",
            [shape(2, KDIM, 256, dtype=BF), shape(2304, 128, dtype=BF)],
            [VM, VM, VM],
            [pltpu.VMEM((2, 64, 256), F32)],
            flops=600_000_000,
        )(cam_shares, slope, turned)
        got = lax.ppermute(send, "c", SWAP)
        mine, joined, latent_part = call(
            mine_kernel,
            "backward_mine",
            [shape(2304, 128), shape(8, 256), shape(2, 256)],
            [VM, VM, VM, VM],
            flops=600_000_000,
        )(turned, pre_grad, cam_shares, join_weight)

    with jax.named_scope("conv_scatter"):
        (packed,) = call(
            pack_kernel,
            "pack",
            [shape(32, 80, 128, dtype=BF)],
            [SM, VM, VM, VM, VM, VM],
            [pltpu.VMEM((16, 128), F32)],
        )(place, mine, got, joined, latent_part, latent_grad)
        blocks = lax.all_to_all(packed, BLOCK, 0, 0)

    with jax.named_scope("conv_middle"):
        middle, rest = call(
            middle_kernel,
            "middle",
            [shape(4, 80, 128, dtype=BF), shape(16, 384, dtype=BF)],
            [SM, VM],
            [pltpu.VMEM((16, 384), F32)],
        )(place, blocks)
        lines = lax.all_to_all(middle, "zh", 0, 0)

    with jax.named_scope("conv_gather"):
        (summed,) = call(finish_kernel, "finish", [shape(32, 80, 128, dtype=BF)], [VM])(lines)
        own = lax.all_to_all(summed, BLOCK, 0, 0)
        other = lax.ppermute(own, "c", SWAP)
        begun, latent = spread(
            spread_own_kernel, "spread_own", [shape(9, 256, 256), shape(2, 256)], [SM, VM], {}
        )(place, own)

    with jax.named_scope("end"):
        rest_other = lax.ppermute(rest, "c", SWAP)
        conv_grad, join_grad = spread(
            spread_other_kernel, "spread_other", [shape(9, 256, 256), shape(64, 256)], [SM, VM, VM, VM, HBM], {4: 0}
        )(place, other, rest, rest_other, begun)
    return (latent, conv_grad, join_grad)


def solution(mesh):
    fine = Mesh(mesh.devices.reshape(2, 4, 2, 4, 4), ("zl", "x", "c", "zh", "y"))
    frame, cam = ("zl", "x", "c"), ("zh", "y")
    in_specs = (
        P(frame, cam, None, None, None),
        P(),
        P(cam, None),
        P(frame, None),
        P(frame, None),
    )
    out_specs = (P(frame, None), P(), P(cam + frame, None))
    return jax.shard_map(on_device, mesh=fine, in_specs=in_specs, out_specs=out_specs, check_vma=False)
```

```python
import functools

import jax
import jax.numpy as jnp
from jax import lax
from jax.experimental import pallas as pl
from jax.experimental.pallas import tpu as pltpu
from jax.sharding import Mesh, PartitionSpec as P

BF = jnp.bfloat16
F32 = jnp.float32
SWAP = [(0, 1), (1, 0)]
BLOCK = ("zl", "x", "y")
KDIM = 768

VM = pl.BlockSpec(memory_space=pltpu.VMEM)
HBM = pl.BlockSpec(memory_space=pltpu.HBM)


def params():
    return pltpu.CompilerParams(vmem_limit_bytes=48 * 1024 * 1024)


def dot(a, b):
    return jnp.dot(a, b, preferred_element_type=F32)


def edge_masks(rows):
    column = lax.broadcasted_iota(jnp.int32, (rows, 256), 0) % 32
    return column != 0, column != 31


def forward_kernel(
    valid_hbm, grad_hbm, join_hbm, maps_hbm, conv_hbm,
    out_ref, slope_ref, turned_ref,
    valid_ref, grad_ref, join_ref, maps_ref, conv_ref, rows_ref, sems,
):
    loads = [
        pltpu.make_async_copy(source, target, sems.at[i])
        for i, (source, target) in enumerate(
            (
                (valid_hbm, valid_ref),
                (grad_hbm, grad_ref),
                (join_hbm, join_ref),
                (maps_hbm, maps_ref),
                (conv_hbm, conv_ref),
            )
        )
    ]
    for load in loads:
        load.start()
    core, cam = lax.axis_index("c"), lax.axis_index("zh") * 4 + lax.axis_index("y")
    loads[0].wait()
    valid = valid_ref[...].astype(F32)
    count = jnp.sum(valid, axis=1, keepdims=True)
    lane = lax.broadcasted_iota(jnp.int32, (2, 176), 1)
    weight = [jnp.sum(jnp.where(lane == cam * 11 + c, valid, 0.0), axis=1, keepdims=True) / count for c in range(11)]
    n = 11 * 32
    not_first, not_last = edge_masks(n)

    loads[1].wait()
    loads[2].wait()
    grad = grad_ref[...]
    for pos in range(4):
        part = lax.dot_general(
            grad, join_ref[256 * pos : 256 * pos + 256, :], (((1,), (1,)), ((), ())), preferred_element_type=F32
        )
        for j in range(2):
            rows_ref[4 * j + pos : 4 * j + pos + 1, :] = part[j : j + 1]
    out_ref[:, 0:8, :] = jnp.broadcast_to(rows_ref[0:8, :].astype(BF)[None], (16, 8, 256))

    loads[3].wait()
    loads[4].wait()
    for f in range(2):
        at = f * 11
        top = maps_ref[at : at + 11, 0:32, :].reshape(n, 256)
        low = maps_ref[at : at + 11, 32:64, :].reshape(n, 256)
        for r in range(2):
            taps = [
                dot(top, conv_ref[(1 - r) * 3 + dx]) + dot(low, conv_ref[(2 - r) * 3 + dx])
                for dx in range(3)
            ]
            pre = taps[1]
            pre = pre + jnp.where(not_first, pltpu.roll(taps[0], 1, 0), 0.0)
            pre = pre + jnp.where(not_last, pltpu.roll(taps[2], n - 1, 0), 0.0)
            sigma = jax.nn.sigmoid(pre)
            feature = pre * sigma
            slope = sigma * (1.0 + pre * (1.0 - sigma))
            pooled = jnp.zeros((32, 256), F32)
            for c in range(11):
                scale = weight[c][f : f + 1]
                rows = slice(32 * c, 32 * c + 32)
                pooled = pooled + feature[rows] * scale
                slope_ref[at + c, 32 * r : 32 * r + 32, :] = slope[rows] * scale
            for k in range(8):
                start = 8 * (8 * r + k) + 4 * f
                rows_ref[start : start + 4, :] = pooled[4 * k : 4 * k + 4]
    out_ref[:, 8:16, :] = rows_ref[...].reshape(16, 8, 256).astype(BF)

    m = 22 * 32
    keep_first, keep_last = edge_masks(m)
    for r in range(2):
        rows = maps_ref[:, 32 * r : 32 * r + 32, :].reshape(m, 256).astype(F32)
        for dx in range(3):
            if dx == 0:
                shifted = jnp.where(keep_first, pltpu.roll(rows, 1, 0), 0.0)
            elif dx == 1:
                shifted = rows
            else:
                shifted = jnp.where(keep_last, pltpu.roll(rows, m - 1, 0), 0.0)
            shifted = jnp.concatenate([shifted, jnp.zeros((KDIM - m, 256), F32)], 0)
            turned = shifted.T.astype(BF)
            for half in range(2):
                slot = core if half == 0 else 1 - core
                start = pl.multiple_of(slot * 384 + dx * 128, 128)
                turned_ref[r, pl.ds(start, 128), :] = turned[128 * half : 128 * half + 128]


def send_kernel(grad_ref, slope_ref, turned_ref, pre_ref, send_ref, grads):
    for k in range(16):
        block = grad_ref[k, 0:8, :].astype(F32)
        for f in range(2):
            grads[f, 4 * k : 4 * k + 4, :] = block[4 * f : 4 * f + 4]
    pre = []
    for r in range(2):
        parts = []
        for f in range(2):
            rows = grads[f, 32 * r : 32 * r + 32, :]
            slope = slope_ref[11 * f : 11 * f + 11, 32 * r : 32 * r + 32, :]
            parts.append((slope * rows[None]).reshape(352, 256).astype(BF))
        parts.append(jnp.zeros((KDIM - 704, 256), BF))
        pre.append(jnp.concatenate(parts, 0))

    for r in range(2):
        pre_ref[r] = pre[r]
    half_taps(turned_ref, pre_ref, 1, send_ref)


def half_taps(turned_ref, pre_ref, slot, out_ref):
    part = slice(384 * slot, 384 * slot + 384)
    top, low = turned_ref[0, part], turned_ref[1, part]
    for dy in range(3):
        if dy == 0:
            value = dot(top, pre_ref[1])
        elif dy == 1:
            value = dot(top, pre_ref[0]) + dot(low, pre_ref[1])
        else:
            value = dot(low, pre_ref[0])
        for dx in range(3):
            for h in range(2):
                s = (dy * 3 + dx) * 2 + h
                out_ref[128 * s : 128 * s + 128, :] = value[
                    128 * dx : 128 * dx + 128, 128 * h : 128 * h + 128
                ].astype(out_ref.dtype)


def mine_kernel(turned_ref, pre_ref, got_ref, join_ref, mine_ref, joined_ref, latent_ref):
    half_taps(turned_ref, pre_ref, 0, mine_ref)
    pooled = jnp.sum(got_ref[:, 8:16, :].astype(F32), axis=0)
    joined = pooled.astype(BF)
    joined_ref[...] = joined.astype(F32)
    parts = [dot(joined, join_ref[256 * pos : 256 * pos + 256, :]) for pos in range(4)]
    for j in range(2):
        latent_ref[j : j + 1, :] = sum(parts[pos][4 * j + pos : 4 * j + pos + 1] for pos in range(4))


def pack_kernel(mine_ref, got_ref, joined_ref, latent_ref, grad_ref, out_ref, last):
    head = (mine_ref[0:2048] + got_ref[0:2048].astype(F32)).astype(BF)
    out_ref[:, 0:64, :] = head.reshape(32, 64, 128)
    foot = mine_ref[2048:2304] + got_ref[2048:2304].astype(F32)
    grad = grad_ref[...].astype(F32)
    last[...] = jnp.zeros((16, 128), F32)
    own_x, own_z = lax.axis_index("x"), lax.axis_index("zl")
    for j in range(2):
        for h in range(2):
            last[11 + 2 * j + h : 12 + 2 * j + h, :] = grad[j : j + 1, 128 * h : 128 * h + 128]
    for z in range(2):
        for x in range(4):
            t = 4 * z + x
            lanes = slice(128 * (t % 2), 128 * (t % 2) + 128)
            for j in range(2):
                row = 4 * j + t // 2
                last[9 + j : 10 + j, :] = joined_ref[row : row + 1, lanes]
            own = jnp.where(jnp.logical_and(own_x == x, own_z == z), 1.0, 0.0)
            for y in range(4):
                b = 4 * t + y
                last[0:8, :] = foot[8 * b : 8 * b + 8]
                last[8:9, :] = latent_ref[y // 2 : y // 2 + 1, 128 * (y % 2) : 128 * (y % 2) + 128] * own
                out_ref[b, 64:80, :] = last[...].astype(BF)


def middle_kernel(got_ref, out_ref, rest_ref, rows_ref):
    head = jnp.sum(got_ref[:, 0:64, :].astype(F32), axis=0).astype(BF)
    foot = jnp.sum(got_ref[:, 64:80, :].astype(F32), axis=0).astype(BF)
    own_y = lax.axis_index("y")
    for z in range(4):
        out_ref[z, 0:64, :] = head
        out_ref[z, 64:80, :] = foot
    for k in range(8):
        last = got_ref[4 * k + own_y, 64:80, :].astype(F32)
        for j in range(2):
            at = slice(2 * k + j, 2 * k + j + 1)
            rows_ref[at, 0:128] = last[9 + j : 10 + j]
            for h in range(2):
                row = 11 + 2 * j + h
                rows_ref[at, 128 + 128 * h : 256 + 128 * h] = last[row : row + 1]
    rest_ref[...] = rows_ref[...].astype(BF)


def finish_kernel(got_ref, out_ref):
    total = jnp.sum(got_ref[...].astype(F32), axis=0).astype(BF)
    for b in range(32):
        out_ref[b] = total


def spread_half(ref, half, conv_hbm, slabs, sem):
    for b in range(32):
        s, i = b // 2, 64 * (b % 2)
        lanes = slice(128 * (s % 2), 128 * (s % 2) + 128)
        slabs[s // 2, i : i + 64, lanes] = ref[b, 0:64, :].astype(F32)
        s, i = b // 16, 8 * (b % 16)
        slabs[8, i : i + 8, 128 * s : 128 * s + 128] = ref[b, 64:80, :].astype(F32)[0:8]
    rows = pl.ds(pl.multiple_of(128 * half, 128), 128)
    copy = pltpu.make_async_copy(slabs, conv_hbm.at[:, rows], sem)
    copy.start()
    return copy


def spread_own_kernel(own_ref, conv_hbm, latent_hbm, slabs, latent_ref, sems):
    copy = spread_half(own_ref, lax.axis_index("c"), conv_hbm, slabs, sems.at[0])
    first = 16 * lax.axis_index("zl") + 4 * lax.axis_index("x")
    for y in range(4):
        row = own_ref[first + y, 64:80, :].astype(F32)[8:9]
        latent_ref[y // 2 : y // 2 + 1, 128 * (y % 2) : 128 * (y % 2) + 128] = row
    small = pltpu.make_async_copy(latent_ref, latent_hbm, sems.at[1])
    small.start()
    copy.wait()
    small.wait()


def spread_other_kernel(other_ref, rest_ref, rest_other_ref, begun_hbm, conv_hbm, join_hbm, slabs, join_ref, sems):
    core = lax.axis_index("c")
    copy = spread_half(other_ref, 1 - core, conv_hbm, slabs, sems.at[0])
    total = jnp.zeros((64, 256), F32)
    for ref in (rest_ref, rest_other_ref):
        rows = ref[...]
        joined = jnp.where(core == 0, rows[:, 0:64], rows[:, 64:128])
        total = total + lax.dot_general(joined, rows[:, 128:384], (((0,), (0,)), ((), ())), preferred_element_type=F32)
    join_ref[...] = total
    small = pltpu.make_async_copy(join_ref, join_hbm, sems.at[1])
    small.start()
    copy.wait()
    small.wait()


def spread(kernel, name, small, in_specs, aliases):
    return pl.pallas_call(
        kernel,
        out_shape=[shape(9, 256, 256), shape(*small)],
        in_specs=in_specs,
        out_specs=[HBM, HBM],
        scratch_shapes=[pltpu.VMEM((9, 128, 256), F32), pltpu.VMEM(small, F32), pltpu.SemaphoreType.DMA((2,))],
        input_output_aliases=aliases,
        compiler_params=params(),
        cost_estimate=pl.CostEstimate(flops=1_000_000, bytes_accessed=2_000_000, transcendentals=0),
        name=name,
    )


def shape(*dims, dtype=F32):
    return jax.ShapeDtypeStruct(dims, dtype)


def call(kernel, name, out_shape, in_specs, scratch=(), flops=1_000_000, moved=3_000_000):
    return pl.pallas_call(
        kernel,
        out_shape=out_shape,
        in_specs=in_specs,
        out_specs=[VM] * len(out_shape),
        scratch_shapes=scratch,
        compiler_params=params(),
        cost_estimate=pl.CostEstimate(flops=flops, bytes_accessed=moved, transcendentals=0),
        name=name,
    )


def in_hbm(array):
    return pltpu.with_memory_space_constraint(array, pltpu.HBM)


def on_device(view_maps, conv_weight, join_weight, valid_cams, latent_grad):
    with jax.named_scope("forward"):
        shares, slope, turned = call(
            forward_kernel,
            "forward",
            [shape(16, 16, 256, dtype=BF), shape(22, 64, 256), shape(2, 768, KDIM, dtype=BF)],
            [HBM, HBM, HBM, HBM, HBM],
            [
                pltpu.VMEM((2, 176), jnp.int32),
                pltpu.VMEM((2, 256), BF),
                pltpu.VMEM((1024, 256), BF),
                pltpu.VMEM((22, 64, 256), BF),
                pltpu.VMEM((9, 256, 256), BF),
                pltpu.VMEM((128, 256), F32),
                pltpu.SemaphoreType.DMA((5,)),
            ],
            flops=1_200_000_000,
        )(*map(in_hbm, (valid_cams, latent_grad, join_weight, view_maps.reshape(22, 64, 256), conv_weight)))
        cam_shares = lax.all_to_all(shares, ("zh", "y"), 0, 0)

    with jax.named_scope("backward"):
        pre_grad, send = call(
            send_kernel,
            "backward_send",
            [shape(2, KDIM, 256, dtype=BF), shape(2304, 128, dtype=BF)],
            [VM, VM, VM],
            [pltpu.VMEM((2, 64, 256), F32)],
            flops=600_000_000,
        )(cam_shares, slope, turned)
        got = lax.ppermute(send, "c", SWAP)
        mine, joined, latent_part = call(
            mine_kernel,
            "backward_mine",
            [shape(2304, 128), shape(8, 256), shape(2, 256)],
            [VM, VM, VM, VM],
            flops=600_000_000,
        )(turned, pre_grad, cam_shares, join_weight)

    with jax.named_scope("conv_scatter"):
        (packed,) = call(
            pack_kernel,
            "pack",
            [shape(32, 80, 128, dtype=BF)],
            [VM, VM, VM, VM, VM],
            [pltpu.VMEM((16, 128), F32)],
        )(mine, got, joined, latent_part, latent_grad)
        blocks = lax.all_to_all(packed, BLOCK, 0, 0)

    with jax.named_scope("conv_middle"):
        middle, rest = call(
            middle_kernel,
            "middle",
            [shape(4, 80, 128, dtype=BF), shape(16, 384, dtype=BF)],
            [VM],
            [pltpu.VMEM((16, 384), F32)],
        )(blocks)
        lines = lax.all_to_all(middle, "zh", 0, 0)

    with jax.named_scope("conv_gather"):
        (summed,) = call(finish_kernel, "finish", [shape(32, 80, 128, dtype=BF)], [VM])(lines)
        own = lax.all_to_all(summed, BLOCK, 0, 0)
        other = lax.ppermute(own, "c", SWAP)
        begun, latent = spread(spread_own_kernel, "spread_own", (2, 256), [VM], {})(own)

    with jax.named_scope("end"):
        rest_other = lax.ppermute(rest, "c", SWAP)
        conv_grad, join_grad = spread(
            spread_other_kernel, "spread_other", (64, 256), [VM, VM, VM, HBM], {3: 0}
        )(other, rest, rest_other, begun)
    return (latent, conv_grad, join_grad)


def solution(mesh):
    fine = Mesh(mesh.devices.reshape(2, 4, 2, 4, 4), ("zl", "x", "c", "zh", "y"))
    frame, cam = ("zl", "x", "c"), ("zh", "y")
    in_specs = (
        P(frame, cam, None, None, None),
        P(),
        P(cam, None),
        P(frame, None),
        P(frame, None),
    )
    out_specs = (P(frame, None), P(), P(cam + frame, None))
    return jax.shard_map(on_device, mesh=fine, in_specs=in_specs, out_specs=out_specs, check_vma=False)
```

```python
import functools

import jax
import jax.numpy as jnp
from jax import lax
from jax.experimental import pallas as pl
from jax.experimental.pallas import tpu as pltpu
from jax.sharding import Mesh, PartitionSpec as P

BF = jnp.bfloat16
F32 = jnp.float32
SWAP = [(0, 1), (1, 0)]
BLOCK = ("zl", "x", "y")
KDIM = 768

VM = pl.BlockSpec(memory_space=pltpu.VMEM)
HBM = pl.BlockSpec(memory_space=pltpu.HBM)


def params():
    return pltpu.CompilerParams(vmem_limit_bytes=48 * 1024 * 1024)


def dot(a, b):
    return jnp.dot(a, b, preferred_element_type=F32)


def edge_masks(rows):
    column = lax.broadcasted_iota(jnp.int32, (rows, 256), 0) % 32
    return column != 0, column != 31


def forward_kernel(
    valid_hbm, grad_hbm, join_hbm, maps_hbm, conv_hbm,
    out_ref, slope_ref, turned_ref,
    valid_ref, grad_ref, join_ref, maps_ref, conv_ref, rows_ref, sems,
):
    loads = [
        pltpu.make_async_copy(source, target, sems.at[i])
        for i, (source, target) in enumerate(
            (
                (maps_hbm, maps_ref),
                (conv_hbm, conv_ref),
                (valid_hbm, valid_ref),
                (join_hbm, join_ref),
                (grad_hbm, grad_ref),
            )
        )
    ]
    for load in loads:
        load.start()
    core, cam = lax.axis_index("c"), lax.axis_index("zh") * 4 + lax.axis_index("y")
    loads[0].wait()
    m = 22 * 32
    keep_first, keep_last = edge_masks(m)
    for r in range(2):
        rows = maps_ref[:, 32 * r : 32 * r + 32, :].reshape(m, 256).astype(F32)
        for dx in range(3):
            if dx == 0:
                shifted = jnp.where(keep_first, pltpu.roll(rows, 1, 0), 0.0)
            elif dx == 1:
                shifted = rows
            else:
                shifted = jnp.where(keep_last, pltpu.roll(rows, m - 1, 0), 0.0)
            shifted = jnp.concatenate([shifted, jnp.zeros((KDIM - m, 256), F32)], 0)
            turned = shifted.astype(BF).T
            for half in range(2):
                slot = core if half == 0 else 1 - core
                start = pl.multiple_of(slot * 384 + dx * 128, 128)
                turned_ref[r, pl.ds(start, 128), :] = turned[128 * half : 128 * half + 128]

    loads[1].wait()
    loads[2].wait()
    valid = valid_ref[...].astype(F32)
    count = jnp.sum(valid, axis=1, keepdims=True)
    lane = lax.broadcasted_iota(jnp.int32, (2, 176), 1)
    weight = [jnp.sum(jnp.where(lane == cam * 11 + c, valid, 0.0), axis=1, keepdims=True) / count for c in range(11)]
    n = 11 * 32
    not_first, not_last = edge_masks(n)

    for f in range(2):
        at = f * 11
        top = maps_ref[at : at + 11, 0:32, :].reshape(n, 256)
        low = maps_ref[at : at + 11, 32:64, :].reshape(n, 256)
        for r in range(2):
            taps = [
                dot(top, conv_ref[(1 - r) * 3 + dx]) + dot(low, conv_ref[(2 - r) * 3 + dx])
                for dx in range(3)
            ]
            pre = taps[1]
            pre = pre + jnp.where(not_first, pltpu.roll(taps[0], 1, 0), 0.0)
            pre = pre + jnp.where(not_last, pltpu.roll(taps[2], n - 1, 0), 0.0)
            sigma = jax.nn.sigmoid(pre)
            feature = pre * sigma
            slope = sigma * (1.0 + pre * (1.0 - sigma))
            pooled = jnp.zeros((32, 256), F32)
            for c in range(11):
                scale = weight[c][f : f + 1]
                rows = slice(32 * c, 32 * c + 32)
                pooled = pooled + feature[rows] * scale
                slope_ref[at + c, 32 * r : 32 * r + 32, :] = slope[rows] * scale
            for k in range(8):
                start = 8 * (8 * r + k) + 4 * f
                rows_ref[start : start + 4, :] = pooled[4 * k : 4 * k + 4]
    out_ref[:, 8:16, :] = rows_ref[...].reshape(16, 8, 256).astype(BF)

    loads[3].wait()
    loads[4].wait()
    grad = grad_ref[...]
    for pos in range(4):
        part = lax.dot_general(
            grad, join_ref[256 * pos : 256 * pos + 256, :], (((1,), (1,)), ((), ())), preferred_element_type=F32
        )
        for j in range(2):
            rows_ref[4 * j + pos : 4 * j + pos + 1, :] = part[j : j + 1]
    out_ref[:, 0:8, :] = jnp.broadcast_to(rows_ref[0:8, :].astype(BF)[None], (16, 8, 256))


def send_kernel(grad_ref, slope_ref, turned_ref, pre_ref, send_ref, grads):
    for k in range(16):
        block = grad_ref[k, 0:8, :].astype(F32)
        for f in range(2):
            grads[f, 4 * k : 4 * k + 4, :] = block[4 * f : 4 * f + 4]
    pre = []
    for r in range(2):
        parts = []
        for f in range(2):
            rows = grads[f, 32 * r : 32 * r + 32, :]
            slope = slope_ref[11 * f : 11 * f + 11, 32 * r : 32 * r + 32, :]
            parts.append((slope * rows[None]).reshape(352, 256).astype(BF))
        parts.append(jnp.zeros((KDIM - 704, 256), BF))
        pre.append(jnp.concatenate(parts, 0))

    for r in range(2):
        pre_ref[r] = pre[r]
    half_taps(turned_ref, pre_ref, 1, send_ref)


def half_taps(turned_ref, pre_ref, slot, out_ref):
    part = slice(384 * slot, 384 * slot + 384)
    top, low = turned_ref[0, part], turned_ref[1, part]
    for dy in range(3):
        if dy == 0:
            value = dot(top, pre_ref[1])
        elif dy == 1:
            value = dot(top, pre_ref[0]) + dot(low, pre_ref[1])
        else:
            value = dot(low, pre_ref[0])
        for dx in range(3):
            for h in range(2):
                s = (dy * 3 + dx) * 2 + h
                out_ref[128 * s : 128 * s + 128, :] = value[
                    128 * dx : 128 * dx + 128, 128 * h : 128 * h + 128
                ].astype(out_ref.dtype)


def mine_kernel(turned_ref, pre_ref, got_ref, join_ref, mine_ref, joined_ref, latent_ref):
    half_taps(turned_ref, pre_ref, 0, mine_ref)
    pooled = jnp.sum(got_ref[:, 8:16, :].astype(F32), axis=0)
    joined = pooled.astype(BF)
    joined_ref[...] = joined.astype(F32)
    parts = [dot(joined, join_ref[256 * pos : 256 * pos + 256, :]) for pos in range(4)]
    for j in range(2):
        latent_ref[j : j + 1, :] = sum(parts[pos][4 * j + pos : 4 * j + pos + 1] for pos in range(4))


def pack_kernel(mine_ref, got_ref, joined_ref, latent_ref, grad_ref, out_ref, last):
    head = (mine_ref[0:2048] + got_ref[0:2048].astype(F32)).astype(BF)
    out_ref[:, 0:64, :] = head.reshape(32, 64, 128)
    foot = mine_ref[2048:2304] + got_ref[2048:2304].astype(F32)
    grad = grad_ref[...].astype(F32)
    last[...] = jnp.zeros((16, 128), F32)
    own_x, own_z = lax.axis_index("x"), lax.axis_index("zl")
    for j in range(2):
        for h in range(2):
            last[11 + 2 * j + h : 12 + 2 * j + h, :] = grad[j : j + 1, 128 * h : 128 * h + 128]
    for z in range(2):
        for x in range(4):
            t = 4 * z + x
            lanes = slice(128 * (t % 2), 128 * (t % 2) + 128)
            for j in range(2):
                row = 4 * j + t // 2
                last[9 + j : 10 + j, :] = joined_ref[row : row + 1, lanes]
            own = jnp.where(jnp.logical_and(own_x == x, own_z == z), 1.0, 0.0)
            for y in range(4):
                b = 4 * t + y
                last[0:8, :] = foot[8 * b : 8 * b + 8]
                last[8:9, :] = latent_ref[y // 2 : y // 2 + 1, 128 * (y % 2) : 128 * (y % 2) + 128] * own
                out_ref[b, 64:80, :] = last[...].astype(BF)


def middle_kernel(got_ref, out_ref, rest_ref, rows_ref):
    head = jnp.sum(got_ref[:, 0:64, :].astype(F32), axis=0).astype(BF)
    foot = jnp.sum(got_ref[:, 64:80, :].astype(F32), axis=0).astype(BF)
    own_y = lax.axis_index("y")
    out_ref[0:64, :] = head
    out_ref[64:80, :] = foot
    for k in range(8):
        last = got_ref[4 * k + own_y, 64:80, :].astype(F32)
        for j in range(2):
            at = slice(2 * k + j, 2 * k + j + 1)
            rows_ref[at, 0:128] = last[9 + j : 10 + j]
            for h in range(2):
                row = 11 + 2 * j + h
                rows_ref[at, 128 + 128 * h : 256 + 128 * h] = last[row : row + 1]
    rest_ref[...] = rows_ref[...].astype(BF)


def finish_kernel(own_ref, one_ref, two_ref, three_ref, out_ref):
    own, one, two, three = (ref[...].astype(F32) for ref in (own_ref, one_ref, two_ref, three_ref))
    total = ((own + two) + (one + three)).astype(BF)
    for b in range(32):
        out_ref[b] = total


def spread_half(ref, half, conv_hbm, slabs, sem):
    for b in range(32):
        s, i = b // 2, 64 * (b % 2)
        lanes = slice(128 * (s % 2), 128 * (s % 2) + 128)
        slabs[s // 2, i : i + 64, lanes] = ref[b, 0:64, :].astype(F32)
        s, i = b // 16, 8 * (b % 16)
        slabs[8, i : i + 8, 128 * s : 128 * s + 128] = ref[b, 64:80, :].astype(F32)[0:8]
    rows = pl.ds(pl.multiple_of(128 * half, 128), 128)
    copy = pltpu.make_async_copy(slabs, conv_hbm.at[:, rows], sem)
    copy.start()
    return copy


def spread_own_kernel(own_ref, conv_hbm, latent_hbm, slabs, latent_ref, sems):
    copy = spread_half(own_ref, lax.axis_index("c"), conv_hbm, slabs, sems.at[0])
    first = 16 * lax.axis_index("zl") + 4 * lax.axis_index("x")
    for y in range(4):
        row = own_ref[first + y, 64:80, :].astype(F32)[8:9]
        latent_ref[y // 2 : y // 2 + 1, 128 * (y % 2) : 128 * (y % 2) + 128] = row
    small = pltpu.make_async_copy(latent_ref, latent_hbm, sems.at[1])
    small.start()
    copy.wait()
    small.wait()


def spread_other_kernel(other_ref, rest_ref, rest_other_ref, begun_hbm, conv_hbm, join_hbm, slabs, join_ref, sems):
    core = lax.axis_index("c")
    copy = spread_half(other_ref, 1 - core, conv_hbm, slabs, sems.at[0])
    total = jnp.zeros((64, 256), F32)
    for ref in (rest_ref, rest_other_ref):
        rows = ref[...]
        joined = jnp.where(core == 0, rows[:, 0:64], rows[:, 64:128])
        total = total + lax.dot_general(joined, rows[:, 128:384], (((0,), (0,)), ((), ())), preferred_element_type=F32)
    join_ref[...] = total
    small = pltpu.make_async_copy(join_ref, join_hbm, sems.at[1])
    small.start()
    copy.wait()
    small.wait()


def spread(kernel, name, small, in_specs, aliases):
    return pl.pallas_call(
        kernel,
        out_shape=[shape(9, 256, 256), shape(*small)],
        in_specs=in_specs,
        out_specs=[HBM, HBM],
        scratch_shapes=[pltpu.VMEM((9, 128, 256), F32), pltpu.VMEM(small, F32), pltpu.SemaphoreType.DMA((2,))],
        input_output_aliases=aliases,
        compiler_params=params(),
        cost_estimate=pl.CostEstimate(flops=1_000_000, bytes_accessed=2_000_000, transcendentals=0),
        name=name,
    )


def shape(*dims, dtype=F32):
    return jax.ShapeDtypeStruct(dims, dtype)


def call(kernel, name, out_shape, in_specs, scratch=(), flops=1_000_000, moved=3_000_000):
    return pl.pallas_call(
        kernel,
        out_shape=out_shape,
        in_specs=in_specs,
        out_specs=[VM] * len(out_shape),
        scratch_shapes=scratch,
        compiler_params=params(),
        cost_estimate=pl.CostEstimate(flops=flops, bytes_accessed=moved, transcendentals=0),
        name=name,
    )


def in_hbm(array):
    return pltpu.with_memory_space_constraint(array, pltpu.HBM)


def on_device(view_maps, conv_weight, join_weight, valid_cams, latent_grad):
    with jax.named_scope("forward"):
        shares, slope, turned = call(
            forward_kernel,
            "forward",
            [shape(16, 16, 256, dtype=BF), shape(22, 64, 256), shape(2, 768, KDIM, dtype=BF)],
            [HBM, HBM, HBM, HBM, HBM],
            [
                pltpu.VMEM((2, 176), jnp.int32),
                pltpu.VMEM((2, 256), BF),
                pltpu.VMEM((1024, 256), BF),
                pltpu.VMEM((22, 64, 256), BF),
                pltpu.VMEM((9, 256, 256), BF),
                pltpu.VMEM((128, 256), F32),
                pltpu.SemaphoreType.DMA((5,)),
            ],
            flops=1_200_000_000,
        )(*map(in_hbm, (valid_cams, latent_grad, join_weight, view_maps.reshape(22, 64, 256), conv_weight)))
        cam_shares = lax.all_to_all(shares, ("zh", "y"), 0, 0)

    with jax.named_scope("backward"):
        pre_grad, send = call(
            send_kernel,
            "backward_send",
            [shape(2, KDIM, 256, dtype=BF), shape(2304, 128, dtype=BF)],
            [VM, VM, VM],
            [pltpu.VMEM((2, 64, 256), F32)],
            flops=600_000_000,
        )(cam_shares, slope, turned)
        got = lax.ppermute(send, "c", SWAP)
        mine, joined, latent_part = call(
            mine_kernel,
            "backward_mine",
            [shape(2304, 128), shape(8, 256), shape(2, 256)],
            [VM, VM, VM, VM],
            flops=600_000_000,
        )(turned, pre_grad, cam_shares, join_weight)

    with jax.named_scope("conv_scatter"):
        (packed,) = call(
            pack_kernel,
            "pack",
            [shape(32, 80, 128, dtype=BF)],
            [VM, VM, VM, VM, VM],
            [pltpu.VMEM((16, 128), F32)],
        )(mine, got, joined, latent_part, latent_grad)
        blocks = lax.all_to_all(packed, BLOCK, 0, 0)

    with jax.named_scope("conv_middle"):
        middle, rest = call(
            middle_kernel,
            "middle",
            [shape(80, 128, dtype=BF), shape(16, 384, dtype=BF)],
            [VM],
            [pltpu.VMEM((16, 384), F32)],
        )(blocks)
        away = [lax.ppermute(middle, "zh", [(i, (i + k) % 4) for i in range(4)]) for k in (1, 2, 3)]

    with jax.named_scope("conv_gather"):
        (summed,) = call(finish_kernel, "finish", [shape(32, 80, 128, dtype=BF)], [VM] * 4)(middle, *away)
        own = lax.all_to_all(summed, BLOCK, 0, 0)
        other = lax.ppermute(own, "c", SWAP)
        begun, latent = spread(spread_own_kernel, "spread_own", (2, 256), [VM], {})(own)

    with jax.named_scope("end"):
        rest_other = lax.ppermute(rest, "c", SWAP)
        conv_grad, join_grad = spread(
            spread_other_kernel, "spread_other", (64, 256), [VM, VM, VM, HBM], {3: 0}
        )(other, rest, rest_other, begun)
    return (latent, conv_grad, join_grad)


def solution(mesh):
    fine = Mesh(mesh.devices.reshape(2, 4, 2, 4, 4), ("zl", "x", "c", "zh", "y"))
    frame, cam = ("zl", "x", "c"), ("zh", "y")
    in_specs = (
        P(frame, cam, None, None, None),
        P(),
        P(cam, None),
        P(frame, None),
        P(frame, None),
    )
    out_specs = (P(frame, None), P(), P(cam + frame, None))
    return jax.shard_map(on_device, mesh=fine, in_specs=in_specs, out_specs=out_specs, check_vma=False)
```

```python
import functools

import jax
import jax.numpy as jnp
from jax import lax
from jax.experimental import pallas as pl
from jax.experimental.pallas import tpu as pltpu
from jax.sharding import Mesh, PartitionSpec as P

BF = jnp.bfloat16
F32 = jnp.float32
SWAP = [(0, 1), (1, 0)]
BLOCK = ("zl", "x", "y")
KDIM = 768

VM = pl.BlockSpec(memory_space=pltpu.VMEM)
HBM = pl.BlockSpec(memory_space=pltpu.HBM)


def params():
    return pltpu.CompilerParams(vmem_limit_bytes=48 * 1024 * 1024)


def dot(a, b):
    return jnp.dot(a, b, preferred_element_type=F32)


def edge_masks(rows):
    column = lax.broadcasted_iota(jnp.int32, (rows, 256), 0) % 32
    return column != 0, column != 31


def forward_kernel(
    valid_hbm, grad_hbm, join_hbm, maps_hbm, conv_hbm,
    out_ref, slope_ref, turned_ref,
    valid_ref, grad_ref, join_ref, maps_ref, conv_ref, rows_ref, sems,
):
    loads = [
        pltpu.make_async_copy(source, target, sems.at[i])
        for i, (source, target) in enumerate(
            (
                (maps_hbm, maps_ref),
                (conv_hbm, conv_ref),
                (valid_hbm, valid_ref),
                (join_hbm, join_ref),
                (grad_hbm, grad_ref),
            )
        )
    ]
    for load in loads:
        load.start()
    core, cam = lax.axis_index("c"), lax.axis_index("zh") * 4 + lax.axis_index("y")
    loads[0].wait()
    m = 22 * 32
    keep_first, keep_last = edge_masks(m)
    for r in range(2):
        rows = maps_ref[:, 32 * r : 32 * r + 32, :].reshape(m, 256).astype(F32)
        for dx in range(3):
            if dx == 0:
                shifted = jnp.where(keep_first, pltpu.roll(rows, 1, 0), 0.0)
            elif dx == 1:
                shifted = rows
            else:
                shifted = jnp.where(keep_last, pltpu.roll(rows, m - 1, 0), 0.0)
            shifted = jnp.concatenate([shifted, jnp.zeros((KDIM - m, 256), F32)], 0)
            turned = shifted.astype(BF).T
            for half in range(2):
                slot = core if half == 0 else 1 - core
                start = pl.multiple_of(slot * 384 + dx * 128, 128)
                turned_ref[r, pl.ds(start, 128), :] = turned[128 * half : 128 * half + 128]

    loads[1].wait()
    loads[2].wait()
    valid = valid_ref[...].astype(F32)
    count = jnp.sum(valid, axis=1, keepdims=True)
    lane = lax.broadcasted_iota(jnp.int32, (2, 176), 1)
    weight = [jnp.sum(jnp.where(lane == cam * 11 + c, valid, 0.0), axis=1, keepdims=True) / count for c in range(11)]
    n = 11 * 32
    not_first, not_last = edge_masks(n)

    for f in range(2):
        at = f * 11
        top = maps_ref[at : at + 11, 0:32, :].reshape(n, 256)
        low = maps_ref[at : at + 11, 32:64, :].reshape(n, 256)
        for r in range(2):
            taps = [
                dot(top, conv_ref[(1 - r) * 3 + dx]) + dot(low, conv_ref[(2 - r) * 3 + dx])
                for dx in range(3)
            ]
            pre = taps[1]
            pre = pre + jnp.where(not_first, pltpu.roll(taps[0], 1, 0), 0.0)
            pre = pre + jnp.where(not_last, pltpu.roll(taps[2], n - 1, 0), 0.0)
            sigma = jax.nn.sigmoid(pre)
            feature = pre * sigma
            slope = sigma * (1.0 + pre * (1.0 - sigma))
            pooled = jnp.zeros((32, 256), F32)
            for c in range(11):
                scale = weight[c][f : f + 1]
                rows = slice(32 * c, 32 * c + 32)
                pooled = pooled + feature[rows] * scale
                slope_ref[at + c, 32 * r : 32 * r + 32, :] = slope[rows] * scale
            for k in range(8):
                start = 8 * (8 * r + k) + 4 * f
                rows_ref[start : start + 4, :] = pooled[4 * k : 4 * k + 4]
    out_ref[:, 8:16, :] = rows_ref[...].reshape(16, 8, 256).astype(BF)

    loads[3].wait()
    loads[4].wait()
    grad = grad_ref[...]
    for pos in range(4):
        part = lax.dot_general(
            grad, join_ref[256 * pos : 256 * pos + 256, :], (((1,), (1,)), ((), ())), preferred_element_type=F32
        )
        for j in range(2):
            rows_ref[4 * j + pos : 4 * j + pos + 1, :] = part[j : j + 1]
    out_ref[:, 0:8, :] = jnp.broadcast_to(rows_ref[0:8, :].astype(BF)[None], (16, 8, 256))


def send_kernel(grad_ref, slope_ref, turned_ref, pre_ref, send_ref, grads):
    for k in range(16):
        block = grad_ref[k, 0:8, :].astype(F32)
        for f in range(2):
            grads[f, 4 * k : 4 * k + 4, :] = block[4 * f : 4 * f + 4]
    pre = []
    for r in range(2):
        parts = []
        for f in range(2):
            rows = grads[f, 32 * r : 32 * r + 32, :]
            slope = slope_ref[11 * f : 11 * f + 11, 32 * r : 32 * r + 32, :]
            parts.append((slope * rows[None]).reshape(352, 256).astype(BF))
        parts.append(jnp.zeros((KDIM - 704, 256), BF))
        pre.append(jnp.concatenate(parts, 0))

    for r in range(2):
        pre_ref[r] = pre[r]
    half_taps(turned_ref, pre_ref, 1, send_ref)


def half_taps(turned_ref, pre_ref, slot, out_ref):
    part = slice(384 * slot, 384 * slot + 384)
    top, low = turned_ref[0, part], turned_ref[1, part]
    for dy in range(3):
        if dy == 0:
            value = dot(top, pre_ref[1])
        elif dy == 1:
            value = dot(top, pre_ref[0]) + dot(low, pre_ref[1])
        else:
            value = dot(low, pre_ref[0])
        for dx in range(3):
            for h in range(2):
                s = (dy * 3 + dx) * 2 + h
                out_ref[128 * s : 128 * s + 128, :] = value[
                    128 * dx : 128 * dx + 128, 128 * h : 128 * h + 128
                ].astype(out_ref.dtype)


def mine_kernel(turned_ref, pre_ref, got_ref, join_ref, mine_ref, joined_ref, latent_ref):
    half_taps(turned_ref, pre_ref, 0, mine_ref)
    pooled = jnp.sum(got_ref[:, 8:16, :].astype(F32), axis=0)
    joined = pooled.astype(BF)
    joined_ref[...] = joined.astype(F32)
    parts = [dot(joined, join_ref[256 * pos : 256 * pos + 256, :]) for pos in range(4)]
    for j in range(2):
        latent_ref[j : j + 1, :] = sum(parts[pos][4 * j + pos : 4 * j + pos + 1] for pos in range(4))


def pack_kernel(mine_ref, got_ref, joined_ref, latent_ref, grad_ref, out_ref, latents, others):
    head = (mine_ref[0:2048] + got_ref[0:2048].astype(F32)).astype(BF)
    out_ref[:, 0:64, :] = head.reshape(32, 64, 128)
    foot = mine_ref[2048:2304] + got_ref[2048:2304].astype(F32)
    grad = grad_ref[...].astype(F32)
    latents[...] = jnp.zeros((8, 128), F32)
    others[...] = jnp.zeros((8, 128), F32)
    for j in range(2):
        for h in range(2):
            lanes = slice(128 * h, 128 * h + 128)
            latents[2 * j + h : 2 * j + h + 1, :] = latent_ref[j : j + 1, lanes]
            others[2 + 2 * j + h : 3 + 2 * j + h, :] = grad[j : j + 1, lanes]
    line = lax.axis_index("zl") * 4 + lax.axis_index("x")
    for t in range(8):
        lanes = slice(128 * (t % 2), 128 * (t % 2) + 128)
        for j in range(2):
            row = 4 * j + t // 2
            others[j : j + 1, :] = joined_ref[row : row + 1, lanes]
        last = jnp.where(line == t, latents[...], others[...])
        for y in range(4):
            b = 4 * t + y
            out_ref[b, 64:80, :] = jnp.concatenate([foot[8 * b : 8 * b + 8], last], 0).astype(BF)


def middle_kernel(got_ref, joined_ref, grad_ref, out_ref, rest_ref, rows_ref):
    out_ref[0:64, :] = jnp.sum(got_ref[:, 0:64, :].astype(F32), axis=0).astype(BF)
    line, own_y = lax.axis_index("zl") * 4 + lax.axis_index("x"), lax.axis_index("y")
    foot = jnp.sum(got_ref[:, 64:80, :].astype(F32), axis=0)[0:8]
    latents = got_ref[4 * line, 64:80, :].astype(F32)
    for y in range(1, 4):
        latents = latents + got_ref[4 * line + y, 64:80, :].astype(F32)
    out_ref[64:80, :] = jnp.concatenate([foot, latents[8:16]], 0).astype(BF)
    grad = grad_ref[...].astype(F32)
    for t in range(8):
        last = got_ref[4 * t + own_y, 64:80, :].astype(F32)
        own = line == t
        lanes = slice(128 * (t % 2), 128 * (t % 2) + 128)
        for j in range(2):
            at = slice(2 * t + j, 2 * t + j + 1)
            row = 4 * j + t // 2
            rows_ref[at, 0:128] = jnp.where(own, joined_ref[row : row + 1, lanes], last[8 + j : 9 + j])
            for h in range(2):
                row = 10 + 2 * j + h
                share = grad[j : j + 1, 128 * h : 128 * h + 128]
                rows_ref[at, 128 + 128 * h : 256 + 128 * h] = jnp.where(own, share, last[row : row + 1])
    rest_ref[...] = rows_ref[...].astype(BF)


def finish_kernel(own_ref, one_ref, two_ref, three_ref, out_ref, latent_ref):
    own, one, two, three = (ref[...].astype(F32) for ref in (own_ref, one_ref, two_ref, three_ref))
    total = (own + two) + (one + three)
    latent_ref[...] = total[72:80]
    conv = total[0:72].astype(BF)
    for b in range(32):
        out_ref[b] = conv


def spread_half(ref, half, conv_hbm, slabs, sem):
    for b in range(32):
        s, i = b // 2, 64 * (b % 2)
        lanes = slice(128 * (s % 2), 128 * (s % 2) + 128)
        slabs[s // 2, i : i + 64, lanes] = ref[b, 0:64, :].astype(F32)
        s, i = b // 16, 8 * (b % 16)
        slabs[8, i : i + 8, 128 * s : 128 * s + 128] = ref[b, 64:72, :].astype(F32)
    rows = pl.ds(pl.multiple_of(128 * half, 128), 128)
    copy = pltpu.make_async_copy(slabs, conv_hbm.at[:, rows], sem)
    copy.start()
    return copy


def spread_own_kernel(own_ref, sums_ref, conv_hbm, latent_hbm, slabs, latent_ref, sems):
    copy = spread_half(own_ref, lax.axis_index("c"), conv_hbm, slabs, sems.at[0])
    for j in range(2):
        for h in range(2):
            latent_ref[j : j + 1, 128 * h : 128 * h + 128] = sums_ref[2 * j + h : 2 * j + h + 1]
    small = pltpu.make_async_copy(latent_ref, latent_hbm, sems.at[1])
    small.start()
    copy.wait()
    small.wait()


def spread_other_kernel(other_ref, rest_ref, rest_other_ref, begun_hbm, conv_hbm, join_hbm, slabs, join_ref, sems):
    core = lax.axis_index("c")
    copy = spread_half(other_ref, 1 - core, conv_hbm, slabs, sems.at[0])
    total = jnp.zeros((64, 256), F32)
    for ref in (rest_ref, rest_other_ref):
        rows = ref[...]
        joined = jnp.where(core == 0, rows[:, 0:64], rows[:, 64:128])
        total = total + lax.dot_general(joined, rows[:, 128:384], (((0,), (0,)), ((), ())), preferred_element_type=F32)
    join_ref[...] = total
    small = pltpu.make_async_copy(join_ref, join_hbm, sems.at[1])
    small.start()
    copy.wait()
    small.wait()


def spread(kernel, name, small, in_specs, aliases):
    return pl.pallas_call(
        kernel,
        out_shape=[shape(9, 256, 256), shape(*small)],
        in_specs=in_specs,
        out_specs=[HBM, HBM],
        scratch_shapes=[pltpu.VMEM((9, 128, 256), F32), pltpu.VMEM(small, F32), pltpu.SemaphoreType.DMA((2,))],
        input_output_aliases=aliases,
        compiler_params=params(),
        cost_estimate=pl.CostEstimate(flops=1_000_000, bytes_accessed=2_000_000, transcendentals=0),
        name=name,
    )


def shape(*dims, dtype=F32):
    return jax.ShapeDtypeStruct(dims, dtype)


def call(kernel, name, out_shape, in_specs, scratch=(), flops=1_000_000, moved=3_000_000):
    return pl.pallas_call(
        kernel,
        out_shape=out_shape,
        in_specs=in_specs,
        out_specs=[VM] * len(out_shape),
        scratch_shapes=scratch,
        compiler_params=params(),
        cost_estimate=pl.CostEstimate(flops=flops, bytes_accessed=moved, transcendentals=0),
        name=name,
    )


def in_hbm(array):
    return pltpu.with_memory_space_constraint(array, pltpu.HBM)


def on_device(view_maps, conv_weight, join_weight, valid_cams, latent_grad):
    with jax.named_scope("forward"):
        shares, slope, turned = call(
            forward_kernel,
            "forward",
            [shape(16, 16, 256, dtype=BF), shape(22, 64, 256), shape(2, 768, KDIM, dtype=BF)],
            [HBM, HBM, HBM, HBM, HBM],
            [
                pltpu.VMEM((2, 176), jnp.int32),
                pltpu.VMEM((2, 256), BF),
                pltpu.VMEM((1024, 256), BF),
                pltpu.VMEM((22, 64, 256), BF),
                pltpu.VMEM((9, 256, 256), BF),
                pltpu.VMEM((128, 256), F32),
                pltpu.SemaphoreType.DMA((5,)),
            ],
            flops=1_200_000_000,
        )(*map(in_hbm, (valid_cams, latent_grad, join_weight, view_maps.reshape(22, 64, 256), conv_weight)))
        cam_shares = lax.all_to_all(shares, ("zh", "y"), 0, 0)

    with jax.named_scope("backward"):
        pre_grad, send = call(
            send_kernel,
            "backward_send",
            [shape(2, KDIM, 256, dtype=BF), shape(2304, 128, dtype=BF)],
            [VM, VM, VM],
            [pltpu.VMEM((2, 64, 256), F32)],
            flops=600_000_000,
        )(cam_shares, slope, turned)
        got = lax.ppermute(send, "c", SWAP)
        mine, joined, latent_part = call(
            mine_kernel,
            "backward_mine",
            [shape(2304, 128), shape(8, 256), shape(2, 256)],
            [VM, VM, VM, VM],
            flops=600_000_000,
        )(turned, pre_grad, cam_shares, join_weight)

    with jax.named_scope("conv_scatter"):
        (packed,) = call(
            pack_kernel,
            "pack",
            [shape(32, 80, 128, dtype=BF)],
            [VM, VM, VM, VM, VM],
            [pltpu.VMEM((8, 128), F32), pltpu.VMEM((8, 128), F32)],
        )(mine, got, joined, latent_part, latent_grad)
        blocks = lax.all_to_all(packed, BLOCK, 0, 0)

    with jax.named_scope("conv_middle"):
        middle, rest = call(
            middle_kernel,
            "middle",
            [shape(80, 128, dtype=BF), shape(16, 384, dtype=BF)],
            [VM, VM, VM],
            [pltpu.VMEM((16, 384), F32)],
        )(blocks, joined, latent_grad)
        away = [lax.ppermute(middle, "zh", [(i, (i + k) % 4) for i in range(4)]) for k in (1, 2, 3)]

    with jax.named_scope("conv_gather"):
        summed, latent_sums = call(
            finish_kernel, "finish", [shape(32, 72, 128, dtype=BF), shape(8, 128)], [VM] * 4
        )(middle, *away)
        own = lax.all_to_all(summed, BLOCK, 0, 0)
        other = lax.ppermute(own, "c", SWAP)
        begun, latent = spread(spread_own_kernel, "spread_own", (2, 256), [VM, VM], {})(
            own, latent_sums
        )

    with jax.named_scope("end"):
        rest_other = lax.ppermute(rest, "c", SWAP)
        conv_grad, join_grad = spread(
            spread_other_kernel, "spread_other", (64, 256), [VM, VM, VM, HBM], {3: 0}
        )(other, rest, rest_other, begun)
    return (latent, conv_grad, join_grad)


def solution(mesh):
    fine = Mesh(mesh.devices.reshape(2, 4, 2, 4, 4), ("zl", "x", "c", "zh", "y"))
    frame, cam = ("zl", "x", "c"), ("zh", "y")
    in_specs = (
        P(frame, cam, None, None, None),
        P(),
        P(cam, None),
        P(frame, None),
        P(frame, None),
    )
    out_specs = (P(frame, None), P(), P(cam + frame, None))
    return jax.shard_map(on_device, mesh=fine, in_specs=in_specs, out_specs=out_specs, check_vma=False)
```

```python
import functools

import jax
import jax.numpy as jnp
from jax import lax
from jax.experimental import pallas as pl
from jax.experimental.pallas import tpu as pltpu
from jax.sharding import Mesh, PartitionSpec as P

BF = jnp.bfloat16
F32 = jnp.float32
SWAP = [(0, 1), (1, 0)]
BLOCK = ("zl", "x", "y")
KDIM = 768

VM = pl.BlockSpec(memory_space=pltpu.VMEM)
HBM = pl.BlockSpec(memory_space=pltpu.HBM)


def params():
    return pltpu.CompilerParams(vmem_limit_bytes=48 * 1024 * 1024)


def dot(a, b):
    return jnp.dot(a, b, preferred_element_type=F32)


def edge_masks(rows):
    column = lax.broadcasted_iota(jnp.int32, (rows, 256), 0) % 32
    return column != 0, column != 31


def forward_kernel(
    valid_hbm, grad_hbm, join_hbm, maps_hbm, conv_hbm,
    out_ref, slope_ref, turned_ref,
    valid_ref, grad_ref, join_ref, maps_ref, conv_ref, rows_ref, sems,
):
    loads = [
        pltpu.make_async_copy(source, target, sems.at[i])
        for i, (source, target) in enumerate(
            (
                (maps_hbm, maps_ref),
                (conv_hbm, conv_ref),
                (valid_hbm, valid_ref),
                (join_hbm, join_ref),
                (grad_hbm, grad_ref),
            )
        )
    ]
    for load in loads:
        load.start()
    core, cam = lax.axis_index("c"), lax.axis_index("zh") * 4 + lax.axis_index("y")
    loads[0].wait()
    m = 22 * 32
    keep_first, keep_last = edge_masks(m)
    for r in range(2):
        rows = maps_ref[:, 32 * r : 32 * r + 32, :].reshape(m, 256).astype(F32)
        for dx in range(3):
            if dx == 0:
                shifted = jnp.where(keep_first, pltpu.roll(rows, 1, 0), 0.0)
            elif dx == 1:
                shifted = rows
            else:
                shifted = jnp.where(keep_last, pltpu.roll(rows, m - 1, 0), 0.0)
            shifted = jnp.concatenate([shifted, jnp.zeros((KDIM - m, 256), F32)], 0)
            turned = shifted.astype(BF).T
            for half in range(2):
                slot = core if half == 0 else 1 - core
                start = pl.multiple_of(slot * 384 + dx * 128, 128)
                turned_ref[r, pl.ds(start, 128), :] = turned[128 * half : 128 * half + 128]

    loads[1].wait()
    loads[2].wait()
    valid = valid_ref[...].astype(F32)
    count = jnp.sum(valid, axis=1, keepdims=True)
    lane = lax.broadcasted_iota(jnp.int32, (2, 176), 1)
    weight = [jnp.sum(jnp.where(lane == cam * 11 + c, valid, 0.0), axis=1, keepdims=True) / count for c in range(11)]
    n = 11 * 32
    not_first, not_last = edge_masks(n)

    for f in range(2):
        at = f * 11
        top = maps_ref[at : at + 11, 0:32, :].reshape(n, 256)
        low = maps_ref[at : at + 11, 32:64, :].reshape(n, 256)
        for r in range(2):
            taps = [
                dot(top, conv_ref[(1 - r) * 3 + dx]) + dot(low, conv_ref[(2 - r) * 3 + dx])
                for dx in range(3)
            ]
            pre = taps[1]
            pre = pre + jnp.where(not_first, pltpu.roll(taps[0], 1, 0), 0.0)
            pre = pre + jnp.where(not_last, pltpu.roll(taps[2], n - 1, 0), 0.0)
            sigma = jax.nn.sigmoid(pre)
            feature = pre * sigma
            slope = sigma * (1.0 + pre * (1.0 - sigma))
            pooled = jnp.zeros((32, 256), F32)
            for c in range(11):
                scale = weight[c][f : f + 1]
                rows = slice(32 * c, 32 * c + 32)
                pooled = pooled + feature[rows] * scale
                slope_ref[at + c, 32 * r : 32 * r + 32, :] = slope[rows] * scale
            for k in range(8):
                start = 8 * (8 * r + k) + 4 * f
                rows_ref[start : start + 4, :] = pooled[4 * k : 4 * k + 4]
    out_ref[:, 8:16, :] = rows_ref[...].reshape(16, 8, 256).astype(BF)

    loads[3].wait()
    loads[4].wait()
    grad = grad_ref[...]
    for pos in range(4):
        part = lax.dot_general(
            grad, join_ref[256 * pos : 256 * pos + 256, :], (((1,), (1,)), ((), ())), preferred_element_type=F32
        )
        for j in range(2):
            rows_ref[4 * j + pos : 4 * j + pos + 1, :] = part[j : j + 1]
    out_ref[:, 0:8, :] = jnp.broadcast_to(rows_ref[0:8, :].astype(BF)[None], (16, 8, 256))


def send_kernel(grad_ref, slope_ref, turned_ref, pre_ref, send_ref, grads):
    for k in range(16):
        block = grad_ref[k, 0:8, :].astype(F32)
        for f in range(2):
            grads[f, 4 * k : 4 * k + 4, :] = block[4 * f : 4 * f + 4]
    pre = []
    for r in range(2):
        parts = []
        for f in range(2):
            rows = grads[f, 32 * r : 32 * r + 32, :]
            slope = slope_ref[11 * f : 11 * f + 11, 32 * r : 32 * r + 32, :]
            parts.append((slope * rows[None]).reshape(352, 256).astype(BF))
        parts.append(jnp.zeros((KDIM - 704, 256), BF))
        pre.append(jnp.concatenate(parts, 0))

    for r in range(2):
        pre_ref[r] = pre[r]
    half_taps(turned_ref, pre_ref, 1, send_ref)


def half_taps(turned_ref, pre_ref, slot, out_ref):
    part = slice(384 * slot, 384 * slot + 384)
    top, low = turned_ref[0, part], turned_ref[1, part]
    for dy in range(3):
        if dy == 0:
            value = dot(top, pre_ref[1])
        elif dy == 1:
            value = dot(top, pre_ref[0]) + dot(low, pre_ref[1])
        else:
            value = dot(low, pre_ref[0])
        for dx in range(3):
            for h in range(2):
                s = (dy * 3 + dx) * 2 + h
                out_ref[128 * s : 128 * s + 128, :] = value[
                    128 * dx : 128 * dx + 128, 128 * h : 128 * h + 128
                ].astype(out_ref.dtype)


def mine_kernel(turned_ref, pre_ref, got_ref, join_ref, mine_ref, joined_ref, latent_ref):
    half_taps(turned_ref, pre_ref, 0, mine_ref)
    pooled = jnp.sum(got_ref[:, 8:16, :].astype(F32), axis=0)
    joined = pooled.astype(BF)
    joined_ref[...] = joined.astype(F32)
    parts = [dot(joined, join_ref[256 * pos : 256 * pos + 256, :]) for pos in range(4)]
    for j in range(2):
        latent_ref[j : j + 1, :] = sum(parts[pos][4 * j + pos : 4 * j + pos + 1] for pos in range(4))


def pack_kernel(mine_ref, got_ref, joined_ref, latent_ref, grad_ref, out_ref, latents, others):
    head = (mine_ref[0:2048] + got_ref[0:2048].astype(F32)).astype(BF)
    out_ref[:, 0:64, :] = head.reshape(32, 64, 128)
    foot = mine_ref[2048:2304] + got_ref[2048:2304].astype(F32)
    grad = grad_ref[...].astype(F32)
    latents[...] = jnp.zeros((8, 128), F32)
    others[...] = jnp.zeros((8, 128), F32)
    for j in range(2):
        for h in range(2):
            lanes = slice(128 * h, 128 * h + 128)
            latents[2 * j + h : 2 * j + h + 1, :] = latent_ref[j : j + 1, lanes]
            others[2 + 2 * j + h : 3 + 2 * j + h, :] = grad[j : j + 1, lanes]
    line = lax.axis_index("zl") * 4 + lax.axis_index("x")
    for t in range(8):
        lanes = slice(128 * (t % 2), 128 * (t % 2) + 128)
        for j in range(2):
            row = 4 * j + t // 2
            others[j : j + 1, :] = joined_ref[row : row + 1, lanes]
        last = jnp.where(line == t, latents[...], others[...])
        for y in range(4):
            b = 4 * t + y
            out_ref[b, 64:80, :] = jnp.concatenate([foot[8 * b : 8 * b + 8], last], 0).astype(BF)


def middle_kernel(got_ref, joined_ref, grad_ref, out_ref, rest_ref, rows_ref):
    out_ref[0:64, :] = jnp.sum(got_ref[:, 0:64, :].astype(F32), axis=0).astype(BF)
    line, own_y = lax.axis_index("zl") * 4 + lax.axis_index("x"), lax.axis_index("y")
    foot = jnp.sum(got_ref[:, 64:80, :].astype(F32), axis=0)[0:8]
    latents = got_ref[4 * line, 64:80, :].astype(F32)
    for y in range(1, 4):
        latents = latents + got_ref[4 * line + y, 64:80, :].astype(F32)
    out_ref[64:80, :] = jnp.concatenate([foot, latents[8:16]], 0).astype(BF)
    grad = grad_ref[...].astype(F32)
    for t in range(8):
        last = got_ref[4 * t + own_y, 64:80, :].astype(F32)
        own = line == t
        lanes = slice(128 * (t % 2), 128 * (t % 2) + 128)
        for j in range(2):
            at = slice(2 * t + j, 2 * t + j + 1)
            row = 4 * j + t // 2
            rows_ref[at, 0:128] = jnp.where(own, joined_ref[row : row + 1, lanes], last[8 + j : 9 + j])
            for h in range(2):
                row = 10 + 2 * j + h
                share = grad[j : j + 1, 128 * h : 128 * h + 128]
                rows_ref[at, 128 + 128 * h : 256 + 128 * h] = jnp.where(own, share, last[row : row + 1])
    rest_ref[...] = rows_ref[...].astype(BF)


def finish_kernel(own_ref, one_ref, two_ref, three_ref, out_ref, latent_ref):
    own, one, two, three = (ref[...].astype(F32) for ref in (own_ref, one_ref, two_ref, three_ref))
    total = (own + two) + (one + three)
    latent_ref[...] = total[72:80]
    conv = total[0:72].astype(BF)
    for b in range(32):
        out_ref[b] = conv


def spread_half(ref, half, conv_hbm, slabs, sem):
    for b in range(32):
        s, i = b // 2, 64 * (b % 2)
        lanes = slice(128 * (s % 2), 128 * (s % 2) + 128)
        slabs[s // 2, i : i + 64, lanes] = ref[b, 0:64, :].astype(F32)
        s, i = b // 16, 8 * (b % 16)
        slabs[8, i : i + 8, 128 * s : 128 * s + 128] = ref[b, 64:72, :].astype(F32)
    rows = pl.ds(pl.multiple_of(128 * half, 128), 128)
    copy = pltpu.make_async_copy(slabs, conv_hbm.at[:, rows], sem)
    copy.start()
    return copy


def spread_own_kernel(own_ref, sums_ref, conv_hbm, latent_hbm, slabs, latent_ref, sems):
    copy = spread_half(own_ref, lax.axis_index("c"), conv_hbm, slabs, sems.at[0])
    for j in range(2):
        for h in range(2):
            latent_ref[j : j + 1, 128 * h : 128 * h + 128] = sums_ref[2 * j + h : 2 * j + h + 1]
    small = pltpu.make_async_copy(latent_ref, latent_hbm, sems.at[1])
    small.start()
    copy.wait()
    small.wait()


def spread_other_kernel(other_ref, rest_ref, rest_other_ref, begun_hbm, conv_hbm, join_hbm, slabs, join_ref, sems):
    core = lax.axis_index("c")
    copy = spread_half(other_ref, 1 - core, conv_hbm, slabs, sems.at[0])
    total = jnp.zeros((64, 256), F32)
    for ref in (rest_ref, rest_other_ref):
        rows = ref[...]
        joined = jnp.where(core == 0, rows[:, 0:64], rows[:, 64:128])
        total = total + lax.dot_general(joined, rows[:, 128:384], (((0,), (0,)), ((), ())), preferred_element_type=F32)
    join_ref[...] = total
    small = pltpu.make_async_copy(join_ref, join_hbm, sems.at[1])
    small.start()
    copy.wait()
    small.wait()


def spread(kernel, name, small, in_specs, aliases):
    return pl.pallas_call(
        kernel,
        out_shape=[shape(9, 256, 256), shape(*small)],
        in_specs=in_specs,
        out_specs=[HBM, HBM],
        scratch_shapes=[pltpu.VMEM((9, 128, 256), F32), pltpu.VMEM(small, F32), pltpu.SemaphoreType.DMA((2,))],
        input_output_aliases=aliases,
        compiler_params=params(),
        cost_estimate=pl.CostEstimate(flops=1_000_000, bytes_accessed=2_000_000, transcendentals=0),
        name=name,
    )


def shape(*dims, dtype=F32):
    return jax.ShapeDtypeStruct(dims, dtype)


def call(kernel, name, out_shape, in_specs, scratch=(), flops=1_000_000, moved=3_000_000):
    return pl.pallas_call(
        kernel,
        out_shape=out_shape,
        in_specs=in_specs,
        out_specs=[VM] * len(out_shape),
        scratch_shapes=scratch,
        compiler_params=params(),
        cost_estimate=pl.CostEstimate(flops=flops, bytes_accessed=moved, transcendentals=0),
        name=name,
    )


def in_hbm(array):
    return pltpu.with_memory_space_constraint(array, pltpu.HBM)


def on_device(view_maps, conv_weight, join_weight, valid_cams, latent_grad):
    with jax.named_scope("forward"):
        shares, slope, turned = call(
            forward_kernel,
            "forward",
            [shape(16, 16, 256, dtype=BF), shape(22, 64, 256), shape(2, 768, KDIM, dtype=BF)],
            [HBM, HBM, HBM, HBM, HBM],
            [
                pltpu.VMEM((2, 176), jnp.int32),
                pltpu.VMEM((2, 256), BF),
                pltpu.VMEM((1024, 256), BF),
                pltpu.VMEM((22, 64, 256), BF),
                pltpu.VMEM((9, 256, 256), BF),
                pltpu.VMEM((128, 256), F32),
                pltpu.SemaphoreType.DMA((5,)),
            ],
            flops=1_200_000_000,
        )(*map(in_hbm, (valid_cams, latent_grad, join_weight, view_maps.reshape(22, 64, 256), conv_weight)))
        cam_shares = lax.all_to_all(shares, ("zh", "y"), 0, 0)

    with jax.named_scope("backward"):
        pre_grad, send = call(
            send_kernel,
            "backward_send",
            [shape(2, KDIM, 256, dtype=BF), shape(2304, 128, dtype=BF)],
            [VM, VM, VM],
            [pltpu.VMEM((2, 64, 256), F32)],
            flops=600_000_000,
        )(cam_shares, slope, turned)
        got = lax.ppermute(send, "c", SWAP)
        mine, joined, latent_part = call(
            mine_kernel,
            "backward_mine",
            [shape(2304, 128), shape(8, 256), shape(2, 256)],
            [VM, VM, VM, VM],
            flops=600_000_000,
        )(turned, pre_grad, cam_shares, join_weight)

    with jax.named_scope("conv_scatter"):
        (packed,) = call(
            pack_kernel,
            "pack",
            [shape(32, 80, 128, dtype=BF)],
            [VM, VM, VM, VM, VM],
            [pltpu.VMEM((8, 128), F32), pltpu.VMEM((8, 128), F32)],
        )(mine, got, joined, latent_part, latent_grad)
        blocks = lax.all_to_all(packed, BLOCK, 0, 0)

    with jax.named_scope("conv_middle"):
        middle, rest = call(
            middle_kernel,
            "middle",
            [shape(80, 128, dtype=BF), shape(16, 384, dtype=BF)],
            [VM, VM, VM],
            [pltpu.VMEM((16, 384), F32)],
        )(blocks, joined, latent_grad)
        away = [lax.ppermute(middle, "zh", [(i, i ^ k) for i in range(4)]) for k in (1, 2, 3)]

    with jax.named_scope("conv_gather"):
        summed, latent_sums = call(
            finish_kernel, "finish", [shape(32, 72, 128, dtype=BF), shape(8, 128)], [VM] * 4
        )(middle, *away)
        own = lax.all_to_all(summed, BLOCK, 0, 0)
        other = lax.ppermute(own, "c", SWAP)
        begun, latent = spread(spread_own_kernel, "spread_own", (2, 256), [VM, VM], {})(
            own, latent_sums
        )

    with jax.named_scope("end"):
        rest_other = lax.ppermute(rest, "c", SWAP)
        conv_grad, join_grad = spread(
            spread_other_kernel, "spread_other", (64, 256), [VM, VM, VM, HBM], {3: 0}
        )(other, rest, rest_other, begun)
    return (latent, conv_grad, join_grad)


def solution(mesh):
    fine = Mesh(mesh.devices.reshape(2, 4, 2, 4, 4), ("zl", "x", "c", "zh", "y"))
    frame, cam = ("zl", "x", "c"), ("zh", "y")
    in_specs = (
        P(frame, cam, None, None, None),
        P(),
        P(cam, None),
        P(frame, None),
        P(frame, None),
    )
    out_specs = (P(frame, None), P(), P(cam + frame, None))
    return jax.shard_map(on_device, mesh=fine, in_specs=in_specs, out_specs=out_specs, check_vma=False)
```

```python
import functools

import jax
import jax.numpy as jnp
from jax import lax
from jax.experimental import pallas as pl
from jax.experimental.pallas import tpu as pltpu
from jax.sharding import Mesh, PartitionSpec as P

BF = jnp.bfloat16
F32 = jnp.float32
SWAP = [(0, 1), (1, 0)]
BLOCK = ("zl", "x", "y")
KDIM = 768

VM = pl.BlockSpec(memory_space=pltpu.VMEM)
HBM = pl.BlockSpec(memory_space=pltpu.HBM)


def params():
    return pltpu.CompilerParams(vmem_limit_bytes=48 * 1024 * 1024)


def dot(a, b):
    return jnp.dot(a, b, preferred_element_type=F32)


def edge_masks(rows):
    column = lax.broadcasted_iota(jnp.int32, (rows, 256), 0) % 32
    return column != 0, column != 31


def forward_kernel(
    valid_hbm, grad_hbm, join_hbm, maps_hbm, conv_hbm,
    out_ref, slope_ref, turned_ref,
    valid_ref, grad_ref, join_ref, maps_ref, conv_ref, rows_ref, sems,
):
    loads = [
        pltpu.make_async_copy(source, target, sems.at[i])
        for i, (source, target) in enumerate(
            (
                (maps_hbm, maps_ref),
                (conv_hbm, conv_ref),
                (valid_hbm, valid_ref),
                (join_hbm, join_ref),
                (grad_hbm, grad_ref),
            )
        )
    ]
    for load in loads:
        load.start()
    core, cam = lax.axis_index("c"), lax.axis_index("zh") * 4 + lax.axis_index("y")
    loads[0].wait()
    m = 22 * 32
    keep_first, keep_last = edge_masks(m)
    for r in range(2):
        rows = maps_ref[:, 32 * r : 32 * r + 32, :].reshape(m, 256).astype(F32)
        for dx in range(3):
            if dx == 0:
                shifted = jnp.where(keep_first, pltpu.roll(rows, 1, 0), 0.0)
            elif dx == 1:
                shifted = rows
            else:
                shifted = jnp.where(keep_last, pltpu.roll(rows, m - 1, 0), 0.0)
            shifted = jnp.concatenate([shifted, jnp.zeros((KDIM - m, 256), F32)], 0)
            turned = shifted.astype(BF).T
            for half in range(2):
                slot = core if half == 0 else 1 - core
                start = pl.multiple_of(slot * 384 + dx * 128, 128)
                turned_ref[r, pl.ds(start, 128), :] = turned[128 * half : 128 * half + 128]

    loads[1].wait()
    loads[2].wait()
    valid = valid_ref[...].astype(F32)
    count = jnp.sum(valid, axis=1, keepdims=True)
    lane = lax.broadcasted_iota(jnp.int32, (2, 176), 1)
    weight = [jnp.sum(jnp.where(lane == cam * 11 + c, valid, 0.0), axis=1, keepdims=True) / count for c in range(11)]
    n = 11 * 32
    not_first, not_last = edge_masks(n)

    for f in range(2):
        at = f * 11
        top = maps_ref[at : at + 11, 0:32, :].reshape(n, 256)
        low = maps_ref[at : at + 11, 32:64, :].reshape(n, 256)
        for r in range(2):
            taps = [
                dot(top, conv_ref[(1 - r) * 3 + dx]) + dot(low, conv_ref[(2 - r) * 3 + dx])
                for dx in range(3)
            ]
            pre = taps[1]
            pre = pre + jnp.where(not_first, pltpu.roll(taps[0], 1, 0), 0.0)
            pre = pre + jnp.where(not_last, pltpu.roll(taps[2], n - 1, 0), 0.0)
            sigma = jax.nn.sigmoid(pre)
            feature = pre * sigma
            slope = sigma * (1.0 + pre * (1.0 - sigma))
            pooled = jnp.zeros((32, 256), F32)
            for c in range(11):
                scale = weight[c][f : f + 1]
                rows = slice(32 * c, 32 * c + 32)
                pooled = pooled + feature[rows] * scale
                slope_ref[at + c, 32 * r : 32 * r + 32, :] = slope[rows] * scale
            for k in range(8):
                start = 8 * (8 * r + k) + 4 * f
                rows_ref[start : start + 4, :] = pooled[4 * k : 4 * k + 4]
    out_ref[:, 8:16, :] = rows_ref[...].reshape(16, 8, 256).astype(BF)

    loads[3].wait()
    loads[4].wait()
    grad = grad_ref[...]
    for pos in range(4):
        part = lax.dot_general(
            grad, join_ref[256 * pos : 256 * pos + 256, :], (((1,), (1,)), ((), ())), preferred_element_type=F32
        )
        for j in range(2):
            rows_ref[4 * j + pos : 4 * j + pos + 1, :] = part[j : j + 1]
    out_ref[:, 0:8, :] = jnp.broadcast_to(rows_ref[0:8, :].astype(BF)[None], (16, 8, 256))


def send_kernel(grad_ref, slope_ref, turned_ref, pre_ref, send_ref, grads):
    for k in range(16):
        block = grad_ref[k, 0:8, :].astype(F32)
        for f in range(2):
            grads[f, 4 * k : 4 * k + 4, :] = block[4 * f : 4 * f + 4]
    pre = []
    for r in range(2):
        parts = []
        for f in range(2):
            rows = grads[f, 32 * r : 32 * r + 32, :]
            slope = slope_ref[11 * f : 11 * f + 11, 32 * r : 32 * r + 32, :]
            parts.append((slope * rows[None]).reshape(352, 256).astype(BF))
        parts.append(jnp.zeros((KDIM - 704, 256), BF))
        pre.append(jnp.concatenate(parts, 0))

    for r in range(2):
        pre_ref[r] = pre[r]
    half_taps(turned_ref, pre_ref, 1, send_ref)


def half_taps(turned_ref, pre_ref, slot, out_ref):
    part = slice(384 * slot, 384 * slot + 384)
    top, low = turned_ref[0, part], turned_ref[1, part]
    for dy in range(3):
        if dy == 0:
            value = dot(top, pre_ref[1])
        elif dy == 1:
            value = dot(top, pre_ref[0]) + dot(low, pre_ref[1])
        else:
            value = dot(low, pre_ref[0])
        for dx in range(3):
            for h in range(2):
                s = (dy * 3 + dx) * 2 + h
                out_ref[128 * s : 128 * s + 128, :] = value[
                    128 * dx : 128 * dx + 128, 128 * h : 128 * h + 128
                ].astype(out_ref.dtype)


def mine_kernel(turned_ref, pre_ref, got_ref, join_ref, mine_ref, joined_ref, latent_ref):
    half_taps(turned_ref, pre_ref, 0, mine_ref)
    pooled = jnp.sum(got_ref[:, 8:16, :].astype(F32), axis=0)
    joined = pooled.astype(BF)
    joined_ref[...] = joined.astype(F32)
    parts = [dot(joined, join_ref[256 * pos : 256 * pos + 256, :]) for pos in range(4)]
    for j in range(2):
        latent_ref[j : j + 1, :] = sum(parts[pos][4 * j + pos : 4 * j + pos + 1] for pos in range(4))


def pack_kernel(mine_ref, got_ref, joined_ref, latent_ref, grad_ref, out_ref, latents, others):
    head = (mine_ref[0:2048] + got_ref[0:2048].astype(F32)).astype(BF)
    out_ref[:, 0:64, :] = head.reshape(32, 64, 128)
    foot = mine_ref[2048:2304] + got_ref[2048:2304].astype(F32)
    grad = grad_ref[...].astype(F32)
    latents[...] = jnp.zeros((8, 128), F32)
    others[...] = jnp.zeros((8, 128), F32)
    for j in range(2):
        for h in range(2):
            lanes = slice(128 * h, 128 * h + 128)
            latents[2 * j + h : 2 * j + h + 1, :] = latent_ref[j : j + 1, lanes]
            others[2 + 2 * j + h : 3 + 2 * j + h, :] = grad[j : j + 1, lanes]
    line = lax.axis_index("zl") * 4 + lax.axis_index("x")
    for t in range(8):
        lanes = slice(128 * (t % 2), 128 * (t % 2) + 128)
        for j in range(2):
            row = 4 * j + t // 2
            others[j : j + 1, :] = joined_ref[row : row + 1, lanes]
        last = jnp.where(line == t, latents[...], others[...])
        for y in range(4):
            b = 4 * t + y
            out_ref[b, 64:80, :] = jnp.concatenate([foot[8 * b : 8 * b + 8], last], 0).astype(BF)


def middle_kernel(got_ref, joined_ref, grad_ref, out_ref, rest_ref, rows_ref):
    out_ref[0:64, :] = jnp.sum(got_ref[:, 0:64, :].astype(F32), axis=0).astype(BF)
    line, own_y = lax.axis_index("zl") * 4 + lax.axis_index("x"), lax.axis_index("y")
    foot = jnp.sum(got_ref[:, 64:80, :].astype(F32), axis=0)[0:8]
    latents = got_ref[4 * line, 64:80, :].astype(F32)
    for y in range(1, 4):
        latents = latents + got_ref[4 * line + y, 64:80, :].astype(F32)
    out_ref[64:80, :] = jnp.concatenate([foot, latents[8:16]], 0).astype(BF)
    grad = grad_ref[...].astype(F32)
    for t in range(8):
        last = got_ref[4 * t + own_y, 64:80, :].astype(F32)
        own = line == t
        lanes = slice(128 * (t % 2), 128 * (t % 2) + 128)
        for j in range(2):
            at = slice(2 * t + j, 2 * t + j + 1)
            row = 4 * j + t // 2
            rows_ref[at, 0:128] = jnp.where(own, joined_ref[row : row + 1, lanes], last[8 + j : 9 + j])
            for h in range(2):
                row = 10 + 2 * j + h
                share = grad[j : j + 1, 128 * h : 128 * h + 128]
                rows_ref[at, 128 + 128 * h : 256 + 128 * h] = jnp.where(own, share, last[row : row + 1])
    rest_ref[...] = rows_ref[...].astype(BF)


def finish_kernel(own_ref, one_ref, two_ref, three_ref, rest_ref, rest_other_ref, out_ref, latent_ref, both_ref):
    both_ref[0] = rest_ref[...]
    both_ref[1] = rest_other_ref[...]
    own, one, two, three = (ref[...].astype(F32) for ref in (own_ref, one_ref, two_ref, three_ref))
    total = (own + two) + (one + three)
    latent_ref[...] = total[72:80]
    conv = total[0:72].astype(BF)
    for b in range(32):
        out_ref[b] = conv


def spread_half(ref, half, conv_hbm, slabs, sem):
    for b in range(32):
        s, i = b // 2, 64 * (b % 2)
        lanes = slice(128 * (s % 2), 128 * (s % 2) + 128)
        slabs[s // 2, i : i + 64, lanes] = ref[b, 0:64, :].astype(F32)
        s, i = b // 16, 8 * (b % 16)
        slabs[8, i : i + 8, 128 * s : 128 * s + 128] = ref[b, 64:72, :].astype(F32)
    rows = pl.ds(pl.multiple_of(128 * half, 128), 128)
    copy = pltpu.make_async_copy(slabs, conv_hbm.at[:, rows], sem)
    copy.start()
    return copy


def spread_own_kernel(own_ref, sums_ref, conv_hbm, latent_hbm, slabs, latent_ref, sems):
    copy = spread_half(own_ref, lax.axis_index("c"), conv_hbm, slabs, sems.at[0])
    for j in range(2):
        for h in range(2):
            latent_ref[j : j + 1, 128 * h : 128 * h + 128] = sums_ref[2 * j + h : 2 * j + h + 1]
    small = pltpu.make_async_copy(latent_ref, latent_hbm, sems.at[1])
    small.start()
    copy.wait()
    small.wait()


def spread_other_kernel(other_ref, both_ref, begun_hbm, conv_hbm, join_hbm, slabs, join_ref, sems):
    core = lax.axis_index("c")
    copy = spread_half(other_ref, 1 - core, conv_hbm, slabs, sems.at[0])
    total = jnp.zeros((64, 256), F32)
    for half in range(2):
        rows = both_ref[half]
        joined = jnp.where(core == 0, rows[:, 0:64], rows[:, 64:128])
        total = total + lax.dot_general(joined, rows[:, 128:384], (((0,), (0,)), ((), ())), preferred_element_type=F32)
    join_ref[...] = total
    small = pltpu.make_async_copy(join_ref, join_hbm, sems.at[1])
    small.start()
    copy.wait()
    small.wait()


def spread(kernel, name, small, in_specs, aliases):
    return pl.pallas_call(
        kernel,
        out_shape=[shape(9, 256, 256), shape(*small)],
        in_specs=in_specs,
        out_specs=[HBM, HBM],
        scratch_shapes=[pltpu.VMEM((9, 128, 256), F32), pltpu.VMEM(small, F32), pltpu.SemaphoreType.DMA((2,))],
        input_output_aliases=aliases,
        compiler_params=params(),
        cost_estimate=pl.CostEstimate(flops=1_000_000, bytes_accessed=2_000_000, transcendentals=0),
        name=name,
    )


def shape(*dims, dtype=F32):
    return jax.ShapeDtypeStruct(dims, dtype)


def call(kernel, name, out_shape, in_specs, scratch=(), flops=1_000_000, moved=3_000_000):
    return pl.pallas_call(
        kernel,
        out_shape=out_shape,
        in_specs=in_specs,
        out_specs=[VM] * len(out_shape),
        scratch_shapes=scratch,
        compiler_params=params(),
        cost_estimate=pl.CostEstimate(flops=flops, bytes_accessed=moved, transcendentals=0),
        name=name,
    )


def in_hbm(array):
    return pltpu.with_memory_space_constraint(array, pltpu.HBM)


def on_device(view_maps, conv_weight, join_weight, valid_cams, latent_grad):
    with jax.named_scope("forward"):
        shares, slope, turned = call(
            forward_kernel,
            "forward",
            [shape(16, 16, 256, dtype=BF), shape(22, 64, 256), shape(2, 768, KDIM, dtype=BF)],
            [HBM, HBM, HBM, HBM, HBM],
            [
                pltpu.VMEM((2, 176), jnp.int32),
                pltpu.VMEM((2, 256), BF),
                pltpu.VMEM((1024, 256), BF),
                pltpu.VMEM((22, 64, 256), BF),
                pltpu.VMEM((9, 256, 256), BF),
                pltpu.VMEM((128, 256), F32),
                pltpu.SemaphoreType.DMA((5,)),
            ],
            flops=1_200_000_000,
        )(*map(in_hbm, (valid_cams, latent_grad, join_weight, view_maps.reshape(22, 64, 256), conv_weight)))
        cam_shares = lax.all_to_all(shares, ("zh", "y"), 0, 0)

    with jax.named_scope("backward"):
        pre_grad, send = call(
            send_kernel,
            "backward_send",
            [shape(2, KDIM, 256, dtype=BF), shape(2304, 128, dtype=BF)],
            [VM, VM, VM],
            [pltpu.VMEM((2, 64, 256), F32)],
            flops=600_000_000,
        )(cam_shares, slope, turned)
        got = lax.ppermute(send, "c", SWAP)
        mine, joined, latent_part = call(
            mine_kernel,
            "backward_mine",
            [shape(2304, 128), shape(8, 256), shape(2, 256)],
            [VM, VM, VM, VM],
            flops=600_000_000,
        )(turned, pre_grad, cam_shares, join_weight)

    with jax.named_scope("conv_scatter"):
        (packed,) = call(
            pack_kernel,
            "pack",
            [shape(32, 80, 128, dtype=BF)],
            [VM, VM, VM, VM, VM],
            [pltpu.VMEM((8, 128), F32), pltpu.VMEM((8, 128), F32)],
        )(mine, got, joined, latent_part, latent_grad)
        blocks = lax.all_to_all(packed, BLOCK, 0, 0)

    with jax.named_scope("conv_middle"):
        middle, rest = call(
            middle_kernel,
            "middle",
            [shape(80, 128, dtype=BF), shape(16, 384, dtype=BF)],
            [VM, VM, VM],
            [pltpu.VMEM((16, 384), F32)],
        )(blocks, joined, latent_grad)
        away = [lax.ppermute(middle, "zh", [(i, i ^ k) for i in range(4)]) for k in (1, 2, 3)]

    with jax.named_scope("conv_gather"):
        rest_other = lax.ppermute(rest, "c", SWAP)
        summed, latent_sums, both = call(
            finish_kernel, "finish", [shape(32, 72, 128, dtype=BF), shape(8, 128), shape(2, 16, 384, dtype=BF)], [VM] * 6
        )(middle, *away, rest, rest_other)
        own = lax.all_to_all(summed, BLOCK, 0, 0)
        other = lax.ppermute(own, "c", SWAP)
        begun, latent = spread(spread_own_kernel, "spread_own", (2, 256), [VM, VM], {})(
            own, latent_sums
        )

    with jax.named_scope("end"):
        conv_grad, join_grad = spread(
            spread_other_kernel, "spread_other", (64, 256), [VM, VM, HBM], {2: 0}
        )(other, both, begun)
    return (latent, conv_grad, join_grad)


def solution(mesh):
    fine = Mesh(mesh.devices.reshape(2, 4, 2, 4, 4), ("zl", "x", "c", "zh", "y"))
    frame, cam = ("zl", "x", "c"), ("zh", "y")
    in_specs = (
        P(frame, cam, None, None, None),
        P(),
        P(cam, None),
        P(frame, None),
        P(frame, None),
    )
    out_specs = (P(frame, None), P(), P(cam + frame, None))
    return jax.shard_map(on_device, mesh=fine, in_specs=in_specs, out_specs=out_specs, check_vma=False)
```
